256 devices in a mesh: group: 8 (over z), dev: 32 (over y, x, core).
Axes of the slice: x: 4, y: 4, z: 8, core: 2. Of those that a mesh axis runs over, the one named last changes fastest.
Arguments:
- hidden_acts: bfloat16 [32768, 11008], P(('group', 'dev')), may hold values from -6 to 6
- out_grads: bfloat16 [32768, 4096], P(('group', 'dev')), may hold values from -6 to 6
- doc_index: int32 [256, 128], P(('group', 'dev')), may hold values from 0 to 31, never falling along the last dimension, each value on 1 to 8 neighbouring positions
- proj_hidden: bfloat16 [128, 11008], replicated, may hold values from -0.0546875 to 0.0546875
- proj_grad: bfloat16 [64, 4096], replicated, may hold values from -0.09375 to 0.09375
Outputs:
- coefficients: float32 [8192, 256], P(('group', 'dev'))
- basis: float32 [256, 8192], P(None, 'dev')
The draws below stay inside these ranges and needn't reach their ends.
Inputs may be any that keep to these rules, and one draw needn't show every extreme that they name: `doc_index`: each row holds, for one device's tokens in order, document numbers that never fall; each of the 32 documents has 1 to 8 tokens.
All inputs are finite; a program needn't handle non-finite values.
Results may differ from the reference program's by a relative error of at most 0.00035.
Values sent between devices are 32-bit elements; how exact they have to be, the bound alone decides.
A program may use at most 128 MiB of HBM per device.

```python
import math
import jax
import jax.numpy as jnp
import numpy as np
from jax import lax

D = 4096
FF = 11008
K_IN = 128
K_OUT = 64
RANK = 256
ITERS = 2
TOK_DEV = 128
DOC_DEV = 32
COLS = 8192
TOKENS = 32768
N_GROUP = 8
N_DEV = 32


def block_levels(key, dims, cuts, smallest, largest):
    gain = 1.0
    for dim, blocks in cuts:
        draws = jax.random.uniform(jax.random.fold_in(jax.random.fold_in(key, 6), dim), (blocks,), jnp.float32, smallest / len(cuts), largest / len(cuts))
        gain = gain * jnp.repeat(jnp.exp(draws), dims[dim] // blocks).reshape((-1,) + (1,) * (len(dims) - 1 - dim))
    return gain


def split_up(count, total, reach, lean):
    weights = [(1 << 20) // math.isqrt(standing ** lean) + 1 for standing in range(2, count + 1)]
    rest, counts = total - reach - (count - 1), [1] * (count - 1)
    while rest > 0:
        movable = [i for i in range(count - 1) if counts[i] < reach]
        whole, remaining = sum([weights[i] for i in movable]), rest
        for i in movable:
            extra = min(reach - counts[i], max(1, remaining * weights[i] // whole), rest)
            counts[i] = counts[i] + extra
            rest = rest - extra
    return np.array([reach] + counts)


def uneven_parts(own_key, number_of, total, most, lean):
    if number_of == 2:
        one = jax.random.randint(own_key, (), max(1, total - most), min(most, total - 1) + 1)
        return jnp.stack([one, total - one])
    sizes = jnp.asarray(split_up(number_of, total, most, lean), jnp.int32)
    couples = (number_of - 1) // 2
    source_of, sink = sizes[1:1 + 2 * couples:2], sizes[2:2 + 2 * couples:2]
    margin = jnp.minimum(source_of - 1, most - sink)
    moved = jax.random.randint(jax.random.fold_in(own_key, 1), (couples,), 0, 1 << 20) % (margin + 1)
    sizes = sizes.at[1:1 + 2 * couples:2].set(source_of - moved).at[2:2 + 2 * couples:2].set(sink + moved)
    return sizes[jax.random.permutation(jax.random.fold_in(own_key, 2), number_of)]


def gaussian(rng, shape, deviation, reach, cuts=(), held_as=jnp.bfloat16):
    array = jax.random.normal(rng, shape, jnp.float32) * deviation
    if len(cuts) > 0:
        array = block_levels(rng, shape, cuts, -0.22, 0.18) * array
    return jnp.clip(array, min=-reach, max=reach).astype(held_as)


def setup_inputs(seed: int = 0) -> dict:
    seeds = jax.random.split(jax.random.key(seed), 6)
    hidden_acts = gaussian(seeds[0], (TOKENS, FF), 1.0, 6.0, ((0, 256),))
    out_grads = gaussian(seeds[1], (TOKENS, D), 1.0, 6.0, ((0, 256),))
    doc_index = jax.vmap(lambda own: jnp.searchsorted(jnp.cumsum(uneven_parts(own, DOC_DEV, TOK_DEV, 2 * TOK_DEV // DOC_DEV, 1)), jnp.arange(TOK_DEV), side="right"))(jax.random.split(seeds[2], (N_GROUP * N_DEV))).reshape((N_GROUP * N_DEV, TOK_DEV)).astype(jnp.int32)
    proj_hidden = gaussian(seeds[3], (K_IN, FF), FF ** -0.5, 0.0546875)
    proj_grad = gaussian(seeds[4], (K_OUT, D), D ** -0.5, 0.09375)
    return {"hidden_acts": hidden_acts, "out_grads": out_grads, "doc_index": doc_index, "proj_hidden": proj_hidden, "proj_grad": proj_grad}


def matmul(first_factor, second_factor):
    return jnp.dot(first_factor.astype(jnp.float32), second_factor.astype(jnp.float32), precision=lax.Precision.HIGHEST, preferred_element_type=jnp.float32)

def orthonormal(images):
    inner_gram = matmul(images.T, images)
    lower_factor = jnp.linalg.cholesky(inner_gram)
    return lax.linalg.triangular_solve(lower_factor, images, left_side=False, lower=True, transpose_a=True)

def document_rows(hidden_tokens, grad_tokens, token_docs, proj_hidden, proj_grad):
    hidden_side = lax.dot_general(hidden_tokens.astype(jnp.float32), proj_hidden.astype(jnp.float32), (((1,), (1,)), ((), ())), preferred_element_type=jnp.float32)
    grad_side = lax.dot_general(grad_tokens.astype(jnp.float32), proj_grad.astype(jnp.float32), (((1,), (1,)), ((), ())), preferred_element_type=jnp.float32)
    one_hot = (token_docs[None, :] == jnp.arange(DOC_DEV, dtype=jnp.int32)[:, None]).astype(jnp.float32)
    weighted = one_hot[:, None, :] * grad_side.T[None, :, :]
    outer_sums = matmul(weighted.reshape(-1, token_docs.shape[0]), hidden_side)
    width_total = grad_side.shape[1] * hidden_side.shape[1]
    return outer_sums.reshape(DOC_DEV, width_total) * (1.0 / math.sqrt(width_total))

def merge_sketch(stacked):
    gram_matrix = matmul(stacked, stacked.T)
    merge_basis = orthonormal(gram_matrix[:, :RANK])
    for repeat in range(ITERS):
        merge_basis = orthonormal(matmul(gram_matrix, merge_basis))
    return matmul(merge_basis.T, stacked)

def reference(hidden_acts, out_grads, doc_index, proj_hidden, proj_grad):
    devices = N_GROUP * N_DEV
    hidden_split = hidden_acts.reshape(devices, TOK_DEV, FF)
    grad_split = out_grads.reshape(devices, TOK_DEV, D)

    def one_device(operands):
        return document_rows(operands[0], operands[1], operands[2], proj_hidden, proj_grad)
    all_rows = lax.map(one_device, (hidden_split, grad_split, doc_index))
    group_rows = all_rows.reshape(N_GROUP, N_DEV * DOC_DEV, COLS)
    sketches = lax.map(merge_sketch, group_rows)
    merged = merge_sketch(sketches.reshape(N_GROUP * RANK, COLS))
    squares = lax.optimization_barrier(jnp.sum(merged * merged, axis=1))
    factors = 1.0 / jnp.sqrt(squares / COLS + 1e-06)
    basis_rows = merged * factors[:, None]
    coefficients = matmul(all_rows.reshape(devices * DOC_DEV, COLS), basis_rows.T) / math.sqrt(COLS)
    return (coefficients, basis_rows)
```

```python
import functools
import math

import jax
import jax.numpy as jnp
from jax import lax
from jax.experimental import pallas as pl
from jax.experimental.pallas import tpu as pltpu
from jax.sharding import PartitionSpec as P

RANK = 256
ITERS = 2
DOC_DEV = 32
F32 = jnp.float32
BF = jnp.bfloat16
MESH = pl.DeviceIdType.MESH
VM = pl.BlockSpec(memory_space=pltpu.VMEM)
HI = lax.Precision.HIGHEST


def split3(x):
    h=x.astype(BF); r=x-h.astype(F32); m=r.astype(BF); l=(r-m.astype(F32)).astype(BF)
    return h,m,l

def panel_factor(P, p, nb):
    n=P.shape[1]
    lane=lax.broadcasted_iota(jnp.int32,(nb,n),1)
    row=lax.broadcasted_iota(jnp.int32,(nb,n),0)
    rowb=lax.broadcasted_iota(jnp.int32,(nb,128),0)
    S=jnp.ones((nb,128),F32)
    for leaf in range(nb//8):
        c0=nb*p+8*leaf
        B=[jnp.broadcast_to(P[:,c0+j:c0+j+1],(nb,128)) for j in range(8)]
        for k in range(8):
            rk=8*leaf+k
            pv=B[k][rk:rk+1,:]
            rp=1.0/pv
            f=jnp.where(rowb>rk,B[k]*rp,0.0)
            for j in range(k+1,8):
                B[j]=B[j]-f*B[j][rk:rk+1,:]
            S=jnp.where(rowb==rk,lax.rsqrt(pv),S)
            hit=lane==(c0+k)
            prow=jnp.where(hit[0:1],1.0,P[rk:rk+1,:])
            ff=jnp.concatenate([f]*(n//128),axis=1)
            P=jnp.where(hit&(row>rk),0.0,jnp.where(hit&(row==rk),1.0,P))-ff*prow
    return P*jnp.concatenate([S]*(n//128),axis=1)

def chol_inv_body(A, nb=32):
    n=A.shape[0]
    for p in range(n//nb):
        r0=nb*p; r1=r0+nb
        R=panel_factor(A[r0:r1,:],p,nb)
        A[r0:r1,:]=R
        if r1<n:
            plane=lax.broadcasted_iota(jnp.int32,(nb,n),1); prow=lax.broadcasted_iota(jnp.int32,(nb,n),0)
            R=jnp.where((plane>=r0)&(plane<r1)&(plane-r0>prow),0.0,R)
            h,m,l=split3(R)
            rhs=jnp.concatenate([h,m,h,l,m,h],axis=0)
            lh,lm,ll=h[:,r1:],m[:,r1:],l[:,r1:]
            lhs=jnp.concatenate([lh,lh,lm,lh,lm,ll],axis=0)
            upd=lax.dot_general(lhs,rhs,(((0,),(0,)),((),())),preferred_element_type=F32)
            lane=lax.broadcasted_iota(jnp.int32,(n-r1,n),1)
            T=A[r1:,:]
            A[r1:,:]=jnp.where((lane>=r0)&(lane<r1),0.0,T)-upd

def chol_kernel(nb,k_ref,w_ref,A):
    A[...]=k_ref[...]
    chol_inv_body(A,nb)
    n=A.shape[0]
    r=lax.broadcasted_iota(jnp.int32,(n,n),0); c=lax.broadcasted_iota(jnp.int32,(n,n),1)
    w_ref[...]=jnp.where(c<=r,A[...],0.0)

def chol_inv(K,nb=32):
    n=K.shape[0]
    return pl.pallas_call(functools.partial(chol_kernel,nb),out_shape=jax.ShapeDtypeStruct((n,n),F32),
      in_specs=[pl.BlockSpec(memory_space=pltpu.VMEM)],out_specs=pl.BlockSpec(memory_space=pltpu.VMEM),
      scratch_shapes=[pltpu.VMEM((n,n),F32)],compiler_params=pltpu.CompilerParams(vmem_limit_bytes=32<<20))(K)


def barrier(peers):
    b=pltpu.get_barrier_semaphore()
    for q in peers: pl.semaphore_signal(b,inc=1,device_id=q,device_id_type=MESH)
    pl.semaphore_wait(b,len(peers))

def rcopy(src,dst,ss,rs,dev):
    return pltpu.make_async_remote_copy(src_ref=src,dst_ref=dst,send_sem=ss,recv_sem=rs,device_id=dev,device_id_type=MESH)

def ag_kernel(x_ref,out,ss,rs,ls):
    g=lax.axis_index("group"); me=lax.axis_index("dev")
    core=lax.rem(me,2); x=lax.rem(me//2,4); y=me//8
    hr=x_ref.shape[0]//2
    def did(yy,xx,cc): return (yy*4+xx)*2+cc
    xs=[lax.rem(x+k,4) for k in (1,2,3)]; ys=[lax.rem(y+k,4) for k in (1,2,3)]
    peers=[(g,did(y,a,core)) for a in xs]+[(g,did(b,x,core)) for b in ys]+[(g,did(y,x,1-core))]
    sib=(g,did(y,x,1-core))
    barrier(peers)
    lc=pltpu.make_async_copy(x_ref,out.at[me],ls); lc.start()
    H=[pl.ds(0,hr),pl.ds(hr,hr)]
    sends=[]
    def send(src,owner,h,dev,slot):
        c=rcopy(src,out.at[owner,H[h]],ss.at[len(sends)],rs.at[owner,h],dev); c.start(); sends.append(c)
    for k in range(3):
        send(x_ref.at[H[0]],me,0,(g,did(y,xs[k],core)),0)
        send(x_ref.at[H[1]],me,1,(g,did(ys[k],x,core)),0)
    for k in range(3):
        send(x_ref.at[H[0]],me,0,(g,did(ys[k],x,core)),0)
        send(x_ref.at[H[1]],me,1,(g,did(y,xs[k],core)),0)
    for h in range(2): send(x_ref.at[H[h]],me,h,sib,0)
    def wait(owner,h):
        rcopy(out.at[owner,H[h]],out.at[owner,H[h]],ss.at[0],rs.at[owner,h],sib).wait_recv()
    order=(0,2,1)
    for k in order:
        ox=did(y,xs[k],core); oy=did(ys[k],x,core)
        wait(ox,0)
        for q in range(3): send(out.at[ox,H[0]],ox,0,(g,did(ys[q],x,core)),0)
        send(out.at[ox,H[0]],ox,0,sib,0)
        wait(oy,1)
        for q in range(3): send(out.at[oy,H[1]],oy,1,(g,did(y,xs[q],core)),0)
        send(out.at[oy,H[1]],oy,1,sib,0)
    for k in order:
        ox=did(y,xs[k],core); oy=did(ys[k],x,core)
        wait(oy,0); send(out.at[oy,H[0]],oy,0,sib,0)
        wait(ox,1); send(out.at[ox,H[1]],ox,1,sib,0)
    for k in order:
        for q in order:
            o=did(ys[k],xs[q],core)
            for h in range(2):
                wait(o,h); send(out.at[o,H[h]],o,h,sib,0)
    lc.wait()
    for yy in range(4):
        for xx in range(4):
            for h in range(2): wait(did(yy,xx,1-core),h)
    for c in sends: c.wait_send()

def ag_dev(x,cid):
    r,c=x.shape
    return pl.pallas_call(ag_kernel,out_shape=jax.ShapeDtypeStruct((32,r,c),F32),in_specs=[VM],out_specs=VM,
      scratch_shapes=[pltpu.SemaphoreType.DMA((80,)),pltpu.SemaphoreType.DMA((32,2)),pltpu.SemaphoreType.DMA],
      compiler_params=pltpu.CompilerParams(collective_id=cid,has_side_effects=True,vmem_limit_bytes=48<<20))(x)

def ar_kernel(axis,n,u_ref,out,rbuf,ss,rs,ss2,rs2):
    g=lax.axis_index("group"); d=lax.axis_index("dev")
    me=g if axis=="group" else d
    def dev(i): return (i,d) if axis=="group" else (g,i)
    r=u_ref.shape[0]//n
    b=pltpu.get_barrier_semaphore()
    def sig(k,_):
        pl.semaphore_signal(b,inc=1,device_id=dev(lax.rem(me+k,n)),device_id_type=MESH); return 0
    lax.fori_loop(1,n,sig,0)
    pl.semaphore_wait(b,n-1)
    def rows(i): return pl.ds(pl.multiple_of(i*r,8),r)
    def s1(k,_):
        q=lax.rem(me+k,n)
        rcopy(u_ref.at[rows(q)],rbuf.at[n-k],ss.at[k],rs.at[n-k],dev(q)).start(); return 0
    lax.fori_loop(1,n,s1,0)
    def w1(k,acc):
        rcopy(rbuf.at[k],rbuf.at[k],ss.at[k],rs.at[k],dev(me)).wait_recv()
        return acc+rbuf[k]
    acc=lax.fori_loop(1,n,w1,u_ref[rows(me),:])
    out[rows(me),:]=acc
    def s2(k,_):
        q=lax.rem(me+k,n)
        rcopy(out.at[rows(me)],out.at[rows(me)],ss2.at[k],rs2.at[n-k],dev(q)).start(); return 0
    lax.fori_loop(1,n,s2,0)
    def w2(k,_):
        q=lax.rem(me+k,n)
        rcopy(out.at[rows(q)],out.at[rows(q)],ss.at[k],rs2.at[k],dev(me)).wait_recv(); return 0
    lax.fori_loop(1,n,w2,0)
    def w3(k,_):
        rcopy(u_ref.at[rows(0)],rbuf.at[k],ss.at[k],rs.at[k],dev(me)).wait_send()
        rcopy(u_ref.at[rows(0)],rbuf.at[k],ss2.at[k],rs.at[k],dev(me)).wait_send()
        return 0
    lax.fori_loop(1,n,w3,0)

def ar(u,axis,n,cid):
    R,c=u.shape
    S=pltpu.SemaphoreType.DMA((n,))
    return pl.pallas_call(functools.partial(ar_kernel,axis,n),out_shape=jax.ShapeDtypeStruct((R,c),F32),in_specs=[VM],out_specs=VM,
      scratch_shapes=[pltpu.VMEM((n,R//n,c),F32),S,S,S,S],
      compiler_params=pltpu.CompilerParams(collective_id=cid,has_side_effects=True,vmem_limit_bytes=48<<20))(u)


def rs_kernel(n, u_ref, out, rbuf, ss, rs):
    g = lax.axis_index("group"); me = lax.axis_index("dev")
    r = u_ref.shape[0] // n
    b = pltpu.get_barrier_semaphore()
    def sig(k, _):
        pl.semaphore_signal(b, inc=1, device_id=(g, lax.rem(me + k, n)), device_id_type=MESH); return 0
    lax.fori_loop(1, n, sig, 0)
    pl.semaphore_wait(b, n - 1)
    def rows(i): return pl.ds(pl.multiple_of(i * r, 8), r)
    def s1(k, _):
        q = lax.rem(me + k, n)
        rcopy(u_ref.at[rows(q)], rbuf.at[n - k], ss.at[k], rs.at[n - k], (g, q)).start(); return 0
    lax.fori_loop(1, n, s1, 0)
    def w1(k, acc):
        rcopy(rbuf.at[k], rbuf.at[k], ss.at[k], rs.at[k], (g, me)).wait_recv()
        return acc + rbuf[k]
    out[...] = lax.fori_loop(1, n, w1, u_ref[rows(me), :])
    def w3(k, _):
        rcopy(u_ref.at[rows(0)], rbuf.at[k], ss.at[k], rs.at[k], (g, me)).wait_send(); return 0
    lax.fori_loop(1, n, w3, 0)


def rs_dev(u, n, cid):
    R, c = u.shape
    S = pltpu.SemaphoreType.DMA((n,))
    return pl.pallas_call(functools.partial(rs_kernel, n), out_shape=jax.ShapeDtypeStruct((R // n, c), F32), in_specs=[VM], out_specs=VM,
      scratch_shapes=[pltpu.VMEM((n, R // n, c), F32), S, S],
      compiler_params=pltpu.CompilerParams(collective_id=cid, has_side_effects=True, vmem_limit_bytes=48 << 20))(u)


def mm(a, b, ca=1, cb=0):
    return lax.dot_general(a, b, (((ca,), (cb,)), ((), ())), precision=HI, preferred_element_type=F32)


def on_device(hidden_acts, out_grads, doc_index, proj_hidden, proj_grad):
    g = lax.axis_index("group"); d = lax.axis_index("dev")
    hs = lax.dot_general(hidden_acts, proj_hidden, (((1,), (1,)), ((), ())), preferred_element_type=F32)
    gt = lax.dot_general(proj_grad, out_grads, (((1,), (1,)), ((), ())), preferred_element_type=F32)
    tok = jnp.concatenate([hs, gt, jnp.broadcast_to(doc_index.astype(F32), (8, 128))], axis=0)
    al = ag_dev(tok, 1)
    H = al[:, :128, :]
    Gt = al[:, 128:192, :]
    O = (al[:, 192, None, :] == jnp.arange(DOC_DEV, dtype=F32)[None, :, None]).astype(F32)
    own = (doc_index == jnp.arange(DOC_DEV, dtype=jnp.int32)[:, None]).astype(F32)
    scale = 1.0 / 8192.0
    gsel = lax.dynamic_slice(Gt, (0, 2 * d, 0), (32, 2, 128)) * (1.0 / math.sqrt(8192))
    W = (O[:, :, None, :] * gsel[:, None, :, :]).reshape(32, 64, 128)
    M = lax.dot_general(W, H, (((2,), (1,)), ((0,), (0,))), precision=HI, preferred_element_type=F32).reshape(1024, 256)
    A = mm(hs, H.reshape(4096, 128), 1, 1)
    B = lax.dot_general(gt, Gt, (((0,), (1,)), ((), ())), precision=HI, preferred_element_type=F32).reshape(128, 4096)
    T = mm(own, A * B).reshape(32, 32, 128)
    Gown = lax.dot_general(T, O, (((2,), (2,)), ((1,), (0,))), precision=HI, preferred_element_type=F32)
    Gown = Gown.transpose(1, 0, 2).reshape(32, 1024) * scale
    Yo = Gown[:, :RANK]
    for it in range(ITERS + 1):
        Y = ag_dev(Yo, 2 + it).reshape(1024, RANK)
        Wi = chol_inv(mm(Y, Y, 0, 0))
        Q = mm(Y, Wi, 1, 1)
        if it < ITERS:
            Yo = mm(Gown, Q)
    S = mm(Q, M, 0, 0)
    X = ar(jnp.where(g == 0, S, 0.0), "group", 8, 5).T
    for it in range(ITERS + 1):
        U = ar(mm(S, X), "dev", 32, 6 + 3 * it)
        K = ar(mm(U, U, 0, 0), "group", 8, 7 + 3 * it)
        V = ar(mm(S, U, 0, 0), "group", 8, 8 + 3 * it)
        Wi = chol_inv(K)
        X = mm(V, Wi, 1, 1)
    merged = X.T
    sq = jnp.broadcast_to(jnp.sum(merged * merged, axis=1)[None, None, :], (32, 8, 256))
    cf = mm(M, X).reshape(32, 32, 256)
    red = rs_dev(jnp.concatenate([cf, sq], axis=1).reshape(1280, 256), 32, 20)
    factors = 1.0 / jnp.sqrt(red[32] / 8192.0 + 1e-06)
    return (red[:32] * (factors / math.sqrt(8192))[None, :], merged * factors[:, None])


def solution(mesh):
    return jax.shard_map(
        on_device,
        mesh=mesh,
        in_specs=(
            P(("group", "dev"), None),
            P(("group", "dev"), None),
            P(("group", "dev"), None),
            P(),
            P(),
        ),
        out_specs=(P(("group", "dev"), None), P(None, "dev")),
        check_vma=False,
    )
```

```python
import functools
import math

import jax
import jax.numpy as jnp
from jax import lax
from jax.experimental import pallas as pl
from jax.experimental.pallas import tpu as pltpu
from jax.sharding import PartitionSpec as P

RANK = 256
ITERS = 2
DOC_DEV = 32
F32 = jnp.float32
BF = jnp.bfloat16
MESH = pl.DeviceIdType.MESH
VM = pl.BlockSpec(memory_space=pltpu.VMEM)
HI = lax.Precision.HIGHEST
SPAN = 600.0


def split3(x):
    h=x.astype(BF); r=x-h.astype(F32); m=r.astype(BF); l=(r-m.astype(F32)).astype(BF)
    return h,m,l

def panel_factor(P, p, nb):
    n=P.shape[1]
    lane=lax.broadcasted_iota(jnp.int32,(nb,n),1)
    row=lax.broadcasted_iota(jnp.int32,(nb,n),0)
    rowb=lax.broadcasted_iota(jnp.int32,(nb,128),0)
    S=jnp.ones((nb,128),F32)
    for leaf in range(nb//8):
        c0=nb*p+8*leaf
        B=[jnp.broadcast_to(P[:,c0+j:c0+j+1],(nb,128)) for j in range(8)]
        for k in range(8):
            rk=8*leaf+k
            pv=B[k][rk:rk+1,:]
            rp=1.0/pv
            f=jnp.where(rowb>rk,B[k]*rp,0.0)
            for j in range(k+1,8):
                B[j]=B[j]-f*B[j][rk:rk+1,:]
            S=jnp.where(rowb==rk,lax.rsqrt(pv),S)
            hit=lane==(c0+k)
            prow=jnp.where(hit[0:1],1.0,P[rk:rk+1,:])
            ff=jnp.concatenate([f]*(n//128),axis=1)
            P=jnp.where(hit&(row>rk),0.0,jnp.where(hit&(row==rk),1.0,P))-ff*prow
    return P*jnp.concatenate([S]*(n//128),axis=1)

def chol_inv_body(A, first, last, nb=32):
    n=A.shape[0]
    for p in range(first, last):
        r0=nb*p; r1=r0+nb
        R=panel_factor(A[r0:r1,:],p,nb)
        A[r0:r1,:]=R
        if r1<n:
            plane=lax.broadcasted_iota(jnp.int32,(nb,n),1); prow=lax.broadcasted_iota(jnp.int32,(nb,n),0)
            R=jnp.where((plane>=r0)&(plane<r1)&(plane-r0>prow),0.0,R)
            h,m,l=split3(R)
            rhs=jnp.concatenate([h,m,h,l,m,h],axis=0)
            lh,lm,ll=h[:,r1:],m[:,r1:],l[:,r1:]
            lhs=jnp.concatenate([lh,lh,lm,lh,lm,ll],axis=0)
            upd=lax.dot_general(lhs,rhs,(((0,),(0,)),((),())),preferred_element_type=F32)
            lane=lax.broadcasted_iota(jnp.int32,(n-r1,n),1)
            T=A[r1:,:]
            A[r1:,:]=jnp.where((lane>=r0)&(lane<r1),0.0,T)-upd


def chol_kernel(k_ref, w_ref, A):
    A[...] = k_ref[...]
    chol_inv_body(A, 0, 8)
    r = lax.broadcasted_iota(jnp.int32, (256, 256), 0); c = lax.broadcasted_iota(jnp.int32, (256, 256), 1)
    w_ref[...] = jnp.where(c <= r, A[...], 0.0)


def chol_inv(K):
    return pl.pallas_call(
        chol_kernel, out_shape=jax.ShapeDtypeStruct((256, 256), F32), in_specs=[VM], out_specs=VM,
        scratch_shapes=[pltpu.VMEM((256, 256), F32)], compiler_params=pltpu.CompilerParams(vmem_limit_bytes=32 << 20),
    )(K)


def rcopy(src, dst, ss, rs, dev):
    return pltpu.make_async_remote_copy(src_ref=src, dst_ref=dst, send_sem=ss, recv_sem=rs, device_id=dev, device_id_type=MESH)


def mm(a, b, ca=1, cb=0):
    return lax.dot_general(a, b, (((ca,), (cb,)), ((), ())), precision=HI, preferred_element_type=F32)


def dotb(a, b, ca=1, cb=0):
    return lax.dot_general(a, b, (((ca,), (cb,)), ((), ())), preferred_element_type=F32)


def ds8(i, r):
    return pl.ds(pl.multiple_of(i * r, 8), r)


class Axis:
    def __init__(self, n, me, dev, sent):
        self.n, self.me, self.dev, self.sent = n, me, dev, sent

    def send(self, src, dst, ss, rs, q):
        c = rcopy(src, dst, ss, rs, self.dev(q))
        c.start()
        self.sent.append(c)

    def each(self, f):
        for k in range(1, self.n):
            f(k, lax.rem(self.me + k, self.n))

    def scatter(self, src, buf, ss, rs):
        n, r = self.n, src.shape[0] // self.n
        self.each(lambda k, q: self.send(src.at[ds8(q, r)], buf.at[n - k], ss.at[k], rs.at[n - k], q))

    def gather_sum(self, src, buf, ss, rs):
        r = src.shape[0] // self.n
        acc = src[ds8(self.me, r), :]
        for k in range(1, self.n):
            rcopy(buf.at[k], buf.at[k], ss.at[k], rs.at[k], self.dev(self.me)).wait_recv()
            acc = acc + buf[k]
        return acc

    def spread(self, src, out, r, ss, rs):
        n = self.n
        self.each(lambda k, q: self.send(src, out.at[ds8(self.me, r)], ss.at[k], rs.at[n - k], q))

    def collect(self, out, r, ss, rs):
        self.each(lambda k, q: rcopy(out.at[ds8(q, r)], out.at[ds8(q, r)], ss.at[k], rs.at[k], self.dev(self.me)).wait_recv())


def ag_dev(g, me, x_ref, out, ss, rs, ls):
    core = lax.rem(me, 2); x = lax.rem(me // 2, 4); y = me // 8
    hr = x_ref.shape[0] // 2
    def did(yy, xx): return (g, (yy * 4 + xx) * 2 + core)
    def slot(yy, xx): return core * 16 + yy * 4 + xx
    xs = [lax.rem(x + k, 4) for k in (1, 2, 3)]; ys = [lax.rem(y + k, 4) for k in (1, 2, 3)]
    sib = (g, (y * 4 + x) * 2 + 1 - core)
    mine = slot(y, x)
    lc = pltpu.make_async_copy(x_ref, out.at[mine], ls); lc.start()
    H = [pl.ds(0, hr), pl.ds(hr, hr)]
    sends = []
    def send(src, owner, h, dev):
        c = rcopy(src, out.at[owner, H[h]], ss.at[len(sends)], rs.at[owner, h], dev); c.start(); sends.append(c)
    for k in range(3):
        send(x_ref.at[H[0]], mine, 0, did(y, xs[k]))
        send(x_ref.at[H[1]], mine, 1, did(ys[k], x))
    for k in range(3):
        send(x_ref.at[H[0]], mine, 0, did(ys[k], x))
        send(x_ref.at[H[1]], mine, 1, did(y, xs[k]))
    for h in range(2): send(x_ref.at[H[h]], mine, h, sib)
    def wait(owner, h):
        rcopy(out.at[owner, H[h]], out.at[owner, H[h]], ss.at[0], rs.at[owner, h], sib).wait_recv()
    order = (0, 2, 1)
    for k in order:
        ox = slot(y, xs[k]); oy = slot(ys[k], x)
        wait(ox, 0)
        for q in range(3): send(out.at[ox, H[0]], ox, 0, did(ys[q], x))
        send(out.at[ox, H[0]], ox, 0, sib)
        wait(oy, 1)
        for q in range(3): send(out.at[oy, H[1]], oy, 1, did(y, xs[q]))
        send(out.at[oy, H[1]], oy, 1, sib)
    for k in order:
        ox = slot(y, xs[k]); oy = slot(ys[k], x)
        wait(oy, 0); send(out.at[oy, H[0]], oy, 0, sib)
        wait(ox, 1); send(out.at[ox, H[1]], ox, 1, sib)
    for k in order:
        for q in order:
            o = slot(ys[k], xs[q])
            for h in range(2):
                wait(o, h); send(out.at[o, H[h]], o, h, sib)
    lc.wait()
    def rest(j, c):
        for h in range(2): wait((1 - core) * 16 + j, h)
        return c
    lax.fori_loop(0, 16, rest, 0)
    for c in sends: c.wait_send()


def token_blocks(hs_parts, gt_cat, own3, idx, tokall, b0):
    Hs, Gc = [], []
    for s in range(4):
        Hs.append(split3(tokall[b0 + s, 0:128, :]))
        h, m, l = split3(tokall[b0 + s, 128:192, :])
        Gc.append(jnp.concatenate([h, m, h, l, m, h], axis=0))
    h, m, l = [jnp.concatenate([x[i] for x in Hs], axis=0) for i in range(3)]
    ah, am, al = hs_parts
    A = dotb(jnp.concatenate([ah, am], axis=1), jnp.concatenate([h, h], axis=1), 1, 1)
    A = A + dotb(jnp.concatenate([ah, al], axis=1), jnp.concatenate([m, h], axis=1), 1, 1)
    A = A + dotb(jnp.concatenate([ah, am], axis=1), jnp.concatenate([l, m], axis=1), 1, 1)
    B = dotb(gt_cat, jnp.concatenate(Gc, axis=1))
    th, tm, tl = split3(A * B)
    T = dotb(own3, jnp.concatenate([th, tm, tl], axis=0))
    r4 = lax.broadcasted_iota(jnp.int32, (128, 512), 0).astype(F32)
    marks = jnp.concatenate([tokall[b0 + s, 192:193, :] for s in range(4)], axis=1)
    O4 = (r4 == marks).astype(F32)
    O4b = O4.astype(BF)
    th, tm, tl = split3(T)
    G4 = dotb(th, O4b, 1, 1) + dotb(tm, O4b, 1, 1) + dotb(tl, O4b, 1, 1)
    return G4, O4, Hs


def merge_kernel(hs_in, gt_in, idx_in, coef, basis, state, tok, tokall, M, Gown, ysrc, Y, A, S, X, Z, W0, W0S, UP, SB, HB, UB, U, VP, VB, V, KP, KB, K,
                 CF, CSB, CHB, CB, SQ, SQB, ag_s, ag_r, ag_l, bs, us, ur, us2, ur2, vs, vr, vs2, vr2, ks, kr, ks2, kr2, cs, cr, qs, qr, zs, zr):
    g = lax.axis_index("group"); d = lax.axis_index("dev")
    core = lax.rem(d, 2); p = d // 2
    sib = (g, 2 * p + 1 - core)
    sent = []
    def drain():
        @pl.when(g == 0)
        def _():
            for k in range(1, 8):
                rcopy(Z.at[ds8(0, 32)], Z.at[ds8(0, 32)], zs.at[k], zr.at[0], (g, d)).wait_send()
                rcopy(Z.at[ds8(0, 32)], Z.at[ds8(0, 32)], zs.at[16 + k], zr.at[0], (g, d)).wait_send()
        for c in sent:
            c.wait_send()
    AC = Axis(16, p, lambda i: (g, 2 * i + core), sent)
    AG = Axis(8, g, lambda i: (i, d), sent)
    b = pltpu.get_barrier_semaphore()
    AC.each(lambda k, q: pl.semaphore_signal(b, inc=1, device_id=AC.dev(q), device_id_type=MESH))
    AG.each(lambda k, q: pl.semaphore_signal(b, inc=1, device_id=AG.dev(q), device_id_type=MESH))
    pl.semaphore_signal(b, inc=1, device_id=sib, device_id_type=MESH)
    tok[0:128, :] = hs_in[...]
    tok[128:192, :] = gt_in[...]
    idx = idx_in[0:1, :]
    tok[192:200, :] = jnp.broadcast_to(idx + 32 * lax.rem(p, 4), (8, 128)).astype(F32)
    half = lambda c, n: pl.ds(pl.multiple_of(c * n, 8), n)
    pl.semaphore_wait(b, 23)
    ag_dev(g, d, tok, tokall, ag_s.at[0], ag_r.at[0], ag_l.at[0])
    hs_parts = split3(tok[0:128, :])
    h, m, l = split3(tok[128:192, :].T)
    gt_cat = jnp.concatenate([h, h, m, h, m, l], axis=1)
    drow = lax.broadcasted_iota(jnp.int32, (32, 128), 0)
    own = (jnp.broadcast_to(idx, (32, 128)) == drow).astype(BF)
    own3 = jnp.concatenate([own, own, own], axis=1)
    par = lax.rem(d, 4)
    gbase = pl.multiple_of((d // 4) * 8, 8)
    r8 = lax.broadcasted_iota(jnp.int32, (8, 128), 0)
    def four(q, c):
        G4, O4, Hs = token_blocks(hs_parts, gt_cat, own3, idx, tokall, 4 * q)
        Gown[q] = G4 * (1.0 / 8192)
        for s in range(4):
            g8 = tokall[4 * q + s, pl.ds(128 + gbase, 8), :]
            O1 = O4[32 * s:32 * s + 32, 128 * s:128 * s + 128]
            g0 = jnp.sum(jnp.where(r8 == 2 * par, g8, 0.0), axis=0, keepdims=True)
            g1 = jnp.sum(jnp.where(r8 == 2 * par + 1, g8, 0.0), axis=0, keepdims=True)
            wh, wm, wl = split3(jnp.concatenate([O1 * g0, O1 * g1], axis=0))
            h, m, l = Hs[s]
            mr = dotb(jnp.concatenate([wh, wh, wm, wh, wm, wl], axis=1), jnp.concatenate([h, m, h, l, m, h], axis=0)) * (1.0 / math.sqrt(8192))
            M[ds8(4 * q + s, 32), 0:128] = mr[0:32]
            M[ds8(4 * q + s, 32), 128:256] = mr[32:64]
        return c
    lax.fori_loop(0, 8, four, 0)
    y0, y1 = Gown[0], Gown[4]
    ysrc[0] = jnp.concatenate([(y1 if s % 2 else y0)[:, 32 * (s // 2):32 * (s // 2) + 32] for s in range(8)], axis=1)
    for it in range(3):
        ag_dev(g, d, ysrc.at[it], Y.at[it], ag_s.at[it + 1], ag_r.at[it + 1], ag_l.at[it + 1])
        if it < 2:
            acc = jnp.zeros((32, 256), F32)
            for q in range(8):
                acc = acc + mm(Gown[q], Y[it, 4 * q:4 * q + 4, :, :].reshape(128, 256))
            ysrc[it + 1] = acc
    def zpart(q, acc):
        yb = Y[2, pl.ds(8 * q, 8), :, :].reshape(256, 256)
        return acc + mm(yb, M[ds8(q, 256), :], 0, 0)
    def gram(q, acc):
        yb = Y[2, pl.ds(8 * q, 8), :, :].reshape(256, 256)
        return acc + mm(yb, yb, 0, 0)
    zero = jnp.zeros((256, 256), F32)
    z1 = lax.fori_loop(0, 4, zpart, zero)
    Z[...] = z1
    @pl.when(g == 0)
    def _():
        for k in range(1, 8):
            rcopy(Z.at[ds8(k, 32)], X.at[ds8(k, 32)], zs.at[k], zr.at[0], (k, d)).start()
        X[0:32, :] = Z[0:32, :]
    A[...] = lax.fori_loop(0, 4, gram, zero)
    chol_inv_body(A, 0, 3)
    @pl.when(g > 0)
    def _():
        rcopy(X.at[ds8(g, 32)], X.at[ds8(g, 32)], zs.at[0], zr.at[0], (g, d)).wait_recv()
    AG.spread(X.at[ds8(g, 32)], X, 32, zs.at[pl.ds(8, 8)], zr.at[pl.ds(8, 8)])
    chol_inv_body(A, 3, 8)
    row = lax.broadcasted_iota(jnp.int32, (256, 256), 0); col = lax.broadcasted_iota(jnp.int32, (256, 256), 1)
    tri = col <= row
    diag = jnp.sum(jnp.where(col == row, A[...], 0.0), axis=0, keepdims=True)
    hi = jnp.max(diag, axis=1, keepdims=True); lo = jnp.min(diag, axis=1, keepdims=True)
    W = jnp.where(tri, A[...], 0.0) + jnp.where(hi < SPAN * lo, 0.0, jnp.nan)
    W0S[...] = W
    @pl.when(g == 0)
    def _():
        for k in range(1, 8):
            rcopy(W0S.at[ds8(k, 32)], W0.at[ds8(k, 32)], zs.at[16 + k], zr.at[16], (k, d)).start()
        W0[0:32, :] = W0S[0:32, :]
    S[...] = mm(W, z1)
    AG.collect(X, 32, zs.at[pl.ds(8, 8)], zr.at[pl.ds(8, 8)])
    xt = X[...].T
    for it in range(3):
        UP[it] = mm(S[...], xt)
        to_sib = rcopy(UP.at[it, half(1 - core, 128)], SB.at[it], bs.at[2 * it], bs.at[8 + 2 * it], sib)
        to_sib.start()
        sent.append(to_sib)
        if it == 0:
            @pl.when(g > 0)
            def _():
                rcopy(W0.at[ds8(g, 32)], W0.at[ds8(g, 32)], zs.at[0], zr.at[16], (g, d)).wait_recv()
            AG.spread(W0.at[ds8(g, 32)], W0, 32, zs.at[pl.ds(24, 8)], zr.at[pl.ds(24, 8)])
        to_sib.wait_recv()
        HB[it] = UP[it, half(core, 128), :] + SB[it]
        AC.scatter(HB.at[it], UB.at[it], us.at[it], ur.at[it])
        uh = U.at[it, half(core, 128)]
        uh[ds8(p, 8), :] = AC.gather_sum(HB.at[it], UB.at[it], us.at[it], ur.at[it])
        AC.spread(uh.at[ds8(p, 8)], uh, 8, us2.at[it], ur2.at[it])
        AC.collect(uh, 8, us2.at[it], ur2.at[it])
        swap = rcopy(uh, uh, bs.at[2 * it + 1], bs.at[9 + 2 * it], sib)
        swap.start()
        sent.append(swap)
        swap.wait_recv()
        u = U[it]
        if it == 2:
            mine = core * 16 + p
            KP[...] = mm(u, u, 0, 0)
            KB[ds8(g, 8), :] = KP[ds8(mine, 8), :]
            AG.spread(KP.at[ds8(mine, 8)], KB, 8, ks, kr)
        VP[it] = mm(S[...], u, 0, 0)
        AG.scatter(VP.at[it], VB.at[it], vs.at[it], vr.at[it])
        if it == 2:
            AG.collect(KB, 8, ks, kr)
            acc = KB[0:8, :]
            for q in range(1, 8):
                acc = acc + KB[8 * q:8 * q + 8, :]
            kh = K.at[half(core, 128)]
            kh[ds8(p, 8), :] = acc
            AC.spread(kh.at[ds8(p, 8)], kh, 8, ks2, kr2)
        V[it, ds8(g, 32), :] = AG.gather_sum(VP.at[it], VB.at[it], vs.at[it], vr.at[it])
        AG.spread(V.at[it, ds8(g, 32)], V.at[it], 32, vs2.at[it], vr2.at[it])
        if it == 2:
            AC.collect(kh, 8, ks2, kr2)
            swap_k = rcopy(kh, kh, bs.at[6], bs.at[14], sib)
            swap_k.start()
            sent.append(swap_k)
            swap_k.wait_recv()
            A[...] = K[...]
            chol_inv_body(A, 0, 3)
        AG.collect(V.at[it], 32, vs2.at[it], vr2.at[it])
        if it == 0:
            AG.collect(W0, 32, zs.at[pl.ds(24, 8)], zr.at[pl.ds(24, 8)])
            xt = mm(V[0], W0[...], 1, 1)
        else:
            xt = V[it]
    def cpart(q, c):
        CF[ds8(q, 256), :] = mm(M[ds8(q, 256), :], V[2])
        return c
    lax.fori_loop(0, 4, cpart, 0)
    csib = rcopy(CF.at[half(1 - core, 512)], CSB, bs.at[7], bs.at[15], sib)
    csib.start()
    sent.append(csib)
    chol_inv_body(A, 3, 5)
    csib.wait_recv()
    CHB[...] = CF[half(core, 512), :] + CSB[...]
    AC.scatter(CHB, CB, cs, cr)
    chol_inv_body(A, 5, 8)
    diag = jnp.sum(jnp.where(col == row, A[...], 0.0), axis=0, keepdims=True)
    hi = jnp.max(diag, axis=1, keepdims=True); lo = jnp.min(diag, axis=1, keepdims=True)
    state[...] = jnp.broadcast_to(jnp.where(hi < SPAN * lo, 1.0, 0.0), (8, 128))
    W = jnp.where(tri, A[...], 0.0)
    mt = mm(V[2], W, 1, 1)
    SQ[0] = jnp.broadcast_to(jnp.sum(mt * mt, axis=0, keepdims=True), (8, 256))
    qsib = rcopy(SQ.at[0], SQ.at[1], qs.at[0], qr.at[0], sib)
    qsib.start()
    sent.append(qsib)
    cfs = mm(AC.gather_sum(CHB, CB, cs, cr), W, 1, 1)
    qsib.wait_recv()
    SQB[ds8(p, 8), :] = SQ[0] + SQ[1]
    AC.spread(SQB.at[ds8(p, 8)], SQB, 8, qs, qr)
    AC.collect(SQB, 8, qs, qr)
    sq = SQB[0:8, :]
    for q in range(1, 16):
        sq = sq + SQB[8 * q:8 * q + 8, :]
    f = 1.0 / jnp.sqrt(sq[0:1, :] / 8192.0 + 1e-06)
    coef[...] = cfs * (f * (1.0 / math.sqrt(8192)))
    basis[...] = (mt * f).T
    drain()


def merge_all(hs, gt, idx):
    D = pltpu.SemaphoreType.DMA
    V = lambda *s: pltpu.VMEM(s, F32)
    return pl.pallas_call(
        merge_kernel,
        out_shape=[jax.ShapeDtypeStruct((32, 256), F32), jax.ShapeDtypeStruct((256, 256), F32), jax.ShapeDtypeStruct((8, 128), F32)],
        in_specs=[VM, VM, VM], out_specs=[VM, VM, VM],
        scratch_shapes=[
            V(200, 128), V(32, 200, 128), V(1024, 256), V(8, 32, 128), V(3, 32, 256), V(3, 32, 32, 256),
            V(256, 256), V(256, 256), V(256, 256), V(256, 256), V(256, 256), V(256, 256),
            V(3, 256, 256), V(3, 128, 256), V(3, 128, 256), V(3, 16, 8, 256), V(3, 256, 256), V(3, 256, 256), V(3, 8, 32, 256), V(3, 256, 256),
            V(256, 256), V(64, 256), V(256, 256), V(1024, 256), V(512, 256), V(512, 256), V(16, 32, 256), V(2, 8, 256), V(128, 256),
            D((4, 80)), D((4, 32, 2)), D((4,)), D((16,)),
            D((3, 16)), D((3, 16)), D((3, 16)), D((3, 16)), D((3, 8)), D((3, 8)), D((3, 8)), D((3, 8)),
            D((8,)), D((8,)), D((16,)), D((16,)), D((16,)), D((16,)), D((16,)), D((16,)), D((32,)), D((32,)),
        ],
        compiler_params=pltpu.CompilerParams(collective_id=1, has_side_effects=True, vmem_limit_bytes=56 << 20),
    )(hs, gt, idx)


def merge_slow(hs, gt, doc_index):
    def orth(Y):
        return mm(Y, chol_inv(mm(Y, Y, 0, 0)), 1, 1)
    def sum_parts(x, axis, n):
        r = x.shape[0] // n
        return lax.all_to_all(x, axis, split_axis=0, concat_axis=0, tiled=True).reshape(n, r, x.shape[1]).sum(axis=0)
    def gather(x, axis, n):
        return lax.all_to_all(jnp.tile(x, (n, 1)), axis, split_axis=0, concat_axis=0, tiled=True)
    def total(x):
        return gather(sum_parts(x, "dev", 32), "dev", 32)
    own = (doc_index == jnp.arange(DOC_DEV, dtype=jnp.int32)[:, None]).astype(F32)
    weighted = own[:, None, :] * gt[None, :, :]
    rows = mm(weighted.reshape(-1, 128), hs).reshape(DOC_DEV, 8192) * (1.0 / math.sqrt(8192))
    block = lax.all_to_all(rows, "dev", split_axis=1, concat_axis=0, tiled=True)
    G = total(mm(block, block, 1, 1))
    Q = orth(G[:, :RANK])
    for _ in range(ITERS):
        Q = orth(mm(G, Q))
    stacked = gather(mm(Q, block, 0, 0), "group", 8)
    Q = orth(total(mm(stacked, stacked[:RANK], 1, 1)))
    for _ in range(ITERS):
        Q = orth(total(mm(stacked, mm(stacked, Q, 0, 0))))
    merged = mm(Q, stacked, 0, 0)
    squares = total(jnp.broadcast_to(jnp.sum(merged * merged, axis=1)[None, :], (32, RANK)))[0]
    basis = merged * (1.0 / jnp.sqrt(squares / 8192.0 + 1e-06))[:, None]
    summed = sum_parts(mm(block, basis, 1, 1), "dev", 32)
    return summed / math.sqrt(8192), basis


def on_device(hidden_acts, out_grads, doc_index, proj_hidden, proj_grad):
    hs = lax.dot_general(hidden_acts, proj_hidden, (((1,), (1,)), ((), ())), preferred_element_type=F32)
    gt = lax.dot_general(proj_grad, out_grads, (((1,), (1,)), ((), ())), preferred_element_type=F32)
    coef, basis, state = merge_all(hs, gt, doc_index)
    return lax.cond(state[0, 0] > 0.5, lambda: (coef, basis), lambda: merge_slow(hs, gt, doc_index))


def solution(mesh):
    return jax.shard_map(
        on_device,
        mesh=mesh,
        in_specs=(
            P(("group", "dev"), None),
            P(("group", "dev"), None),
            P(("group", "dev"), None),
            P(),
            P(),
        ),
        out_specs=(P(("group", "dev"), None), P(None, "dev")),
        check_vma=False,
    )
```

```python
import functools
import math

import jax
import jax.numpy as jnp
from jax import lax
from jax.experimental import pallas as pl
from jax.experimental.pallas import tpu as pltpu
from jax.sharding import PartitionSpec as P

RANK = 256
ITERS = 2
DOC_DEV = 32
F32 = jnp.float32
BF = jnp.bfloat16
MESH = pl.DeviceIdType.MESH
VM = pl.BlockSpec(memory_space=pltpu.VMEM)
HI = lax.Precision.HIGHEST
SPAN = 600.0


def split3(x):
    h=x.astype(BF); r=x-h.astype(F32); m=r.astype(BF); l=(r-m.astype(F32)).astype(BF)
    return h,m,l

def panel_factor(P, p, nb):
    n=P.shape[1]
    lane=lax.broadcasted_iota(jnp.int32,(nb,n),1)
    row=lax.broadcasted_iota(jnp.int32,(nb,n),0)
    rowb=lax.broadcasted_iota(jnp.int32,(nb,128),0)
    S=jnp.ones((nb,128),F32)
    for leaf in range(nb//8):
        c0=nb*p+8*leaf
        B=[jnp.broadcast_to(P[:,c0+j:c0+j+1],(nb,128)) for j in range(8)]
        for k in range(8):
            rk=8*leaf+k
            pv=B[k][rk:rk+1,:]
            rp=1.0/pv
            f=jnp.where(rowb>rk,B[k]*rp,0.0)
            for j in range(k+1,8):
                B[j]=B[j]-f*B[j][rk:rk+1,:]
            S=jnp.where(rowb==rk,lax.rsqrt(pv),S)
            hit=lane==(c0+k)
            prow=jnp.where(hit[0:1],1.0,P[rk:rk+1,:])
            ff=jnp.concatenate([f]*(n//128),axis=1)
            P=jnp.where(hit&(row>rk),0.0,jnp.where(hit&(row==rk),1.0,P))-ff*prow
    return P*jnp.concatenate([S]*(n//128),axis=1)

def chol_inv_body(A, first, last, nb=32):
    n=A.shape[0]
    for p in range(first, last):
        r0=nb*p; r1=r0+nb
        R=panel_factor(A[r0:r1,:],p,nb)
        A[r0:r1,:]=R
        if r1<n:
            plane=lax.broadcasted_iota(jnp.int32,(nb,n),1); prow=lax.broadcasted_iota(jnp.int32,(nb,n),0)
            R=jnp.where((plane>=r0)&(plane<r1)&(plane-r0>prow),0.0,R)
            h,m,l=split3(R)
            rhs=jnp.concatenate([h,m,h,l,m,h],axis=0)
            lh,lm,ll=h[:,r1:],m[:,r1:],l[:,r1:]
            lhs=jnp.concatenate([lh,lh,lm,lh,lm,ll],axis=0)
            upd=lax.dot_general(lhs,rhs,(((0,),(0,)),((),())),preferred_element_type=F32)
            lane=lax.broadcasted_iota(jnp.int32,(n-r1,n),1)
            T=A[r1:,:]
            A[r1:,:]=jnp.where((lane>=r0)&(lane<r1),0.0,T)-upd


def chol_kernel(k_ref, w_ref, A):
    A[...] = k_ref[...]
    chol_inv_body(A, 0, 8)
    r = lax.broadcasted_iota(jnp.int32, (256, 256), 0); c = lax.broadcasted_iota(jnp.int32, (256, 256), 1)
    w_ref[...] = jnp.where(c <= r, A[...], 0.0)


def chol_inv(K):
    return pl.pallas_call(
        chol_kernel, out_shape=jax.ShapeDtypeStruct((256, 256), F32), in_specs=[VM], out_specs=VM,
        scratch_shapes=[pltpu.VMEM((256, 256), F32)], compiler_params=pltpu.CompilerParams(vmem_limit_bytes=32 << 20),
    )(K)


def rcopy(src, dst, ss, rs, dev):
    return pltpu.make_async_remote_copy(src_ref=src, dst_ref=dst, send_sem=ss, recv_sem=rs, device_id=dev, device_id_type=MESH)


def mm(a, b, ca=1, cb=0):
    return lax.dot_general(a, b, (((ca,), (cb,)), ((), ())), precision=HI, preferred_element_type=F32)


def dotb(a, b, ca=1, cb=0):
    return lax.dot_general(a, b, (((ca,), (cb,)), ((), ())), preferred_element_type=F32)


def ds8(i, r):
    return pl.ds(pl.multiple_of(i * r, 8), r)


class Axis:
    def __init__(self, n, me, dev, sent):
        self.n, self.me, self.dev, self.sent = n, me, dev, sent

    def send(self, src, dst, ss, rs, q):
        c = rcopy(src, dst, ss, rs, self.dev(q))
        c.start()
        self.sent.append(c)

    def each(self, f):
        h = self.n // 2
        for k in sorted(range(1, self.n), key=lambda k: abs(k - h)):
            f(k, lax.rem(self.me + k, self.n))

    def scatter(self, src, buf, ss, rs):
        n, r = self.n, src.shape[0] // self.n
        self.each(lambda k, q: self.send(src.at[ds8(q, r)], buf.at[n - k], ss.at[k], rs.at[n - k], q))

    def gather_sum(self, src, buf, ss, rs):
        r = src.shape[0] // self.n
        acc = src[ds8(self.me, r), :]
        for k in range(1, self.n):
            rcopy(buf.at[k], buf.at[k], ss.at[k], rs.at[k], self.dev(self.me)).wait_recv()
            acc = acc + buf[k]
        return acc

    def spread(self, src, out, r, ss, rs):
        n = self.n
        self.each(lambda k, q: self.send(src, out.at[ds8(self.me, r)], ss.at[k], rs.at[n - k], q))

    def collect(self, out, r, ss, rs):
        self.each(lambda k, q: rcopy(out.at[ds8(q, r)], out.at[ds8(q, r)], ss.at[k], rs.at[k], self.dev(self.me)).wait_recv())


def ag_tokens(g, me, x_ref, out, ss, rs, ls, sent):
    core = lax.rem(me, 2); x = lax.rem(me // 2, 4); y = me // 8
    def did(yy, xx): return (g, (yy * 4 + xx) * 2 + core)
    def slot(yy, xx): return core * 16 + yy * 4 + xx
    xs = [lax.rem(x + k, 4) for k in (1, 2, 3)]; ys = [lax.rem(y + k, 4) for k in (1, 2, 3)]
    sib = (g, (y * 4 + x) * 2 + 1 - core)
    mine = slot(y, x)
    lc = pltpu.make_async_copy(x_ref, out.at[mine], ls); lc.start()
    H = [pl.ds(0, 104), pl.ds(104, 96)]
    sends = []
    def send(src, owner, h, dev):
        c = rcopy(src, out.at[owner, H[h]], ss.at[len(sends)], rs.at[owner, h], dev); c.start(); sends.append(c)
    for k in range(3):
        send(x_ref.at[H[0]], mine, 0, did(y, xs[k]))
        send(x_ref.at[H[1]], mine, 1, did(ys[k], x))
    for k in range(3):
        send(x_ref.at[H[0]], mine, 0, did(ys[k], x))
        send(x_ref.at[H[1]], mine, 1, did(y, xs[k]))
    for h in range(2): send(x_ref.at[H[h]], mine, h, sib)
    def wait(owner, h):
        rcopy(out.at[owner, H[h]], out.at[owner, H[h]], ss.at[0], rs.at[owner, h], sib).wait_recv()
    order = (0, 2, 1)
    for k in order:
        ox = slot(y, xs[k]); oy = slot(ys[k], x)
        wait(ox, 0)
        for q in range(3): send(out.at[ox, H[0]], ox, 0, did(ys[q], x))
        send(out.at[ox, H[0]], ox, 0, sib)
        wait(oy, 1)
        for q in range(3): send(out.at[oy, H[1]], oy, 1, did(y, xs[q]))
        send(out.at[oy, H[1]], oy, 1, sib)
    for k in order:
        ox = slot(y, xs[k]); oy = slot(ys[k], x)
        wait(oy, 0); send(out.at[oy, H[0]], oy, 0, sib)
        wait(ox, 1); send(out.at[ox, H[1]], ox, 1, sib)
    for k in order:
        for q in order:
            o = slot(ys[k], xs[q])
            for h in range(2):
                wait(o, h); send(out.at[o, H[h]], o, h, sib)
    lc.wait()
    sent.extend(sends)
    def other_core():
        def rest(j, c):
            for h in range(2): wait((1 - core) * 16 + j, h)
            return c
        lax.fori_loop(0, 16, rest, 0)
    return other_core


def ag_block(g, me, x_ref, out, ss, rs, ls, sent, beside=lambda i: None):
    core = lax.rem(me, 2); x = lax.rem(me // 2, 4); y = me // 8
    hr = x_ref.shape[0] // 2
    def did(yy, xx): return (g, (yy * 4 + xx) * 2 + core)
    sib = (g, (y * 4 + x) * 2 + 1 - core)
    lc = pltpu.make_async_copy(x_ref, out.at[core, y, x], ls); lc.start()
    A, B = pl.ds(0, hr), pl.ds(hr, hr)
    def send(src, dst, i, j, dev):
        c = rcopy(src, dst, ss.at[i], rs.at[j], dev); c.start(); sent.append(c)
    def wait(ref, j):
        rcopy(ref, ref, ss.at[0], rs.at[j], sib).wait_recv()
    for k in (1, 3, 2):
        send(x_ref.at[A], out.at[core, y, x, A], k, 4 - k, did(y, lax.rem(x + k, 4)))
        send(x_ref.at[B], out.at[core, y, x, B], 4 + k, 8 - k, did(lax.rem(y + k, 4), x))
    beside(0)
    lc.wait()
    for k in (1, 2, 3): wait(out.at[core, y, lax.rem(x + k, 4), A], k)
    row = out.at[core, y, :, A]
    for k in (1, 3, 2): send(row, row, 8 + k, 12 - k, did(lax.rem(y + k, 4), x))
    for k in (1, 2, 3): wait(out.at[core, lax.rem(y + k, 4), x, B], 4 + k)
    column = out.at[core, :, x, B]
    for k in (1, 3, 2): send(column, column, 12 + k, 16 - k, did(y, lax.rem(x + k, 4)))
    beside(1)
    for k in (1, 2, 3): wait(out.at[core, lax.rem(y + k, 4), :, A], 8 + k)
    send(out.at[core, :, :, A], out.at[core, :, :, A], 0, 0, sib)
    for k in (1, 2, 3): wait(out.at[core, :, lax.rem(x + k, 4), B], 12 + k)
    send(out.at[core, :, :, B], out.at[core, :, :, B], 4, 4, sib)
    beside(2)
    wait(out.at[1 - core, :, :, A], 0)
    wait(out.at[1 - core, :, :, B], 4)


def token_blocks(hs_parts, gt_cat, own3, idx, tokall, b0):
    Hs, Gc = [], []
    for s in range(4):
        Hs.append(split3(tokall[b0 + s, 0:128, :]))
        h, m, l = split3(tokall[b0 + s, 128:192, :])
        Gc.append(jnp.concatenate([h, m, h, l, m, h], axis=0))
    h, m, l = [jnp.concatenate([x[i] for x in Hs], axis=0) for i in range(3)]
    ah, am, al = hs_parts
    A = dotb(jnp.concatenate([ah, am], axis=1), jnp.concatenate([h, h], axis=1), 1, 1)
    A = A + dotb(jnp.concatenate([ah, al], axis=1), jnp.concatenate([m, h], axis=1), 1, 1)
    A = A + dotb(jnp.concatenate([ah, am], axis=1), jnp.concatenate([l, m], axis=1), 1, 1)
    B = dotb(gt_cat, jnp.concatenate(Gc, axis=1))
    th, tm, tl = split3(A * B)
    T = dotb(own3, jnp.concatenate([th, tm, tl], axis=0))
    r4 = lax.broadcasted_iota(jnp.int32, (128, 512), 0).astype(F32)
    marks = jnp.concatenate([tokall[b0 + s, 192:193, :] for s in range(4)], axis=1)
    O4 = (r4 == marks).astype(F32)
    O4b = O4.astype(BF)
    th, tm, tl = split3(T)
    G4 = dotb(th, O4b, 1, 1) + dotb(tm, O4b, 1, 1) + dotb(tl, O4b, 1, 1)
    return G4, O4, Hs


def merge_kernel(hs_in, gt_in, idx_in, coef, basis, state, tok, tokall, M, Gown, ysrc, Y, A, S, X, Z, W0, W0S, UP0, SB0, HB0, UB0, U0,
                 UP, SB, HB, UB, U, VP, VB, V, KP, KB, K, CF, CSB, CHB, CB, SQ, SQB,
                 ag_s, ag_r, ag_l, ys, yr, bs, br, us, ur, us2, ur2, vs, vr, vs2, vr2, ks, kr, ks2, kr2, cs, cr, qs, qr, zs, zr):
    g = lax.axis_index("group"); d = lax.axis_index("dev")
    core = lax.rem(d, 2); p = d // 2
    sib = (g, 2 * p + 1 - core)
    sent = []
    def drain():
        @pl.when(g == 0)
        def _():
            for k in range(1, 8):
                rcopy(Z.at[ds8(0, 32)], Z.at[ds8(0, 32)], zs.at[k], zr.at[0], (g, d)).wait_send()
                rcopy(Z.at[ds8(0, 32)], Z.at[ds8(0, 32)], zs.at[16 + k], zr.at[0], (g, d)).wait_send()
        for c in sent:
            c.wait_send()
    AC = Axis(16, p, lambda i: (g, 2 * i + core), sent)
    AG = Axis(8, g, lambda i: (i, d), sent)
    b = pltpu.get_barrier_semaphore()
    AC.each(lambda k, q: pl.semaphore_signal(b, inc=1, device_id=AC.dev(q), device_id_type=MESH))
    AG.each(lambda k, q: pl.semaphore_signal(b, inc=1, device_id=AG.dev(q), device_id_type=MESH))
    pl.semaphore_signal(b, inc=1, device_id=sib, device_id_type=MESH)
    tok[0:128, :] = hs_in[...]
    tok[128:192, :] = gt_in[...]
    idx = idx_in[0:1, :]
    tok[192:200, :] = jnp.broadcast_to(idx + 32 * lax.rem(p, 4), (8, 128)).astype(F32)
    half = lambda c, n: pl.ds(pl.multiple_of(c * n, 8), n)
    pl.semaphore_wait(b, 23)
    other_core = ag_tokens(g, d, tok, tokall, ag_s, ag_r, ag_l.at[3], sent)
    hs_parts = split3(tok[0:128, :])
    h, m, l = split3(tok[128:192, :].T)
    gt_cat = jnp.concatenate([h, h, m, h, m, l], axis=1)
    drow = lax.broadcasted_iota(jnp.int32, (32, 128), 0)
    own = (jnp.broadcast_to(idx, (32, 128)) == drow).astype(BF)
    own3 = jnp.concatenate([own, own, own], axis=1)
    par = lax.rem(d, 4)
    gbase = pl.multiple_of((d // 4) * 8, 8)
    r8 = lax.broadcasted_iota(jnp.int32, (8, 128), 0)
    def four(q, c):
        G4, O4, Hs = token_blocks(hs_parts, gt_cat, own3, idx, tokall, 4 * q)
        Gown[q] = G4 * (1.0 / 8192)
        for s in range(4):
            g8 = tokall[4 * q + s, pl.ds(128 + gbase, 8), :]
            O1 = O4[32 * s:32 * s + 32, 128 * s:128 * s + 128]
            g0 = jnp.sum(jnp.where(r8 == 2 * par, g8, 0.0), axis=0, keepdims=True)
            g1 = jnp.sum(jnp.where(r8 == 2 * par + 1, g8, 0.0), axis=0, keepdims=True)
            wh, wm, wl = split3(jnp.concatenate([O1 * g0, O1 * g1], axis=0))
            h, m, l = Hs[s]
            mr = dotb(jnp.concatenate([wh, wh, wm, wh, wm, wl], axis=1), jnp.concatenate([h, m, h, l, m, h], axis=0)) * (1.0 / math.sqrt(8192))
            M[ds8(4 * q + s, 32), 0:128] = mr[0:32]
            M[ds8(4 * q + s, 32), 128:256] = mr[32:64]
        return c
    four(4 * core, 0)
    other_core()
    four(4 - 4 * core, 0)
    def later(i):
        def two(j, c):
            return four(4 * j + i + 1, c)
        lax.fori_loop(0, 2, two, 0)
    y0, y1 = Gown[0], Gown[4]
    ysrc[0] = jnp.concatenate([(y1 if s % 2 else y0)[:, 32 * (s // 2):32 * (s // 2) + 32] for s in range(8)], axis=1)
    for it in range(3):
        ag_block(g, d, ysrc.at[it], Y.at[it], ys.at[it], yr.at[it], ag_l.at[it], sent, later if it == 0 else lambda i: None)
        if it < 2:
            acc = jnp.zeros((32, 256), F32)
            for q in range(8):
                acc = acc + mm(Gown[q], Y[it, q // 4, q % 4].reshape(128, 256))
            ysrc[it + 1] = acc
    def zpart(q, acc):
        yb = Y[2, q // 2, pl.ds(2 * lax.rem(q, 2), 2)].reshape(256, 256)
        return acc + mm(yb, M[ds8(q, 256), :], 0, 0)
    def gram(q, acc):
        yb = Y[2, q // 2, pl.ds(2 * lax.rem(q, 2), 2)].reshape(256, 256)
        return acc + mm(yb, yb, 0, 0)
    zero = jnp.zeros((256, 256), F32)
    z1 = lax.fori_loop(0, 4, zpart, zero)
    Z[...] = z1
    @pl.when(g == 0)
    def _():
        for k in range(1, 8):
            rcopy(Z.at[ds8(k, 32)], X.at[ds8(k, 32)], zs.at[k], zr.at[0], (k, d)).start()
        X[0:32, :] = Z[0:32, :]
    A[...] = lax.fori_loop(0, 4, gram, zero)
    chol_inv_body(A, 0, 3)
    @pl.when(g > 0)
    def _():
        rcopy(X.at[ds8(g, 32)], X.at[ds8(g, 32)], zs.at[0], zr.at[0], (g, d)).wait_recv()
    AG.spread(X.at[ds8(g, 32)], X, 32, zs.at[pl.ds(8, 8)], zr.at[pl.ds(8, 8)])
    chol_inv_body(A, 3, 8)
    row = lax.broadcasted_iota(jnp.int32, (256, 256), 0); col = lax.broadcasted_iota(jnp.int32, (256, 256), 1)
    tri = col <= row
    diag = jnp.sum(jnp.where(col == row, A[...], 0.0), axis=0, keepdims=True)
    hi = jnp.max(diag, axis=1, keepdims=True); lo = jnp.min(diag, axis=1, keepdims=True)
    W = jnp.where(tri, A[...], 0.0) + jnp.where(hi < SPAN * lo, 0.0, jnp.nan)
    W0S[...] = W
    @pl.when(g == 0)
    def _():
        for k in range(1, 8):
            rcopy(W0S.at[ds8(k, 32)], W0.at[ds8(k, 32)], zs.at[16 + k], zr.at[16], (k, d)).start()
        W0[0:32, :] = W0S[0:32, :]
    S[...] = mm(W, z1)
    AG.collect(X, 32, zs.at[pl.ds(8, 8)], zr.at[pl.ds(8, 8)])
    xt = X[...].T
    def to_sibling(src, dst, i):
        c = rcopy(src, dst, bs.at[i], br.at[i], sib)
        c.start()
        sent.append(c)
        return c
    UP0[...] = mm(S[...], xt)
    first = to_sibling(UP0.at[half(1 - core, 128)], SB0, 0)
    @pl.when(g > 0)
    def _():
        rcopy(W0.at[ds8(g, 32)], W0.at[ds8(g, 32)], zs.at[0], zr.at[16], (g, d)).wait_recv()
    AG.spread(W0.at[ds8(g, 32)], W0, 32, zs.at[pl.ds(24, 8)], zr.at[pl.ds(24, 8)])
    first.wait_recv()
    HB0[...] = UP0[half(core, 128), :] + SB0[...]
    AC.scatter(HB0, UB0, us.at[4], ur.at[4])
    uh = U0.at[half(core, 128)]
    uh[ds8(p, 8), :] = AC.gather_sum(HB0, UB0, us.at[4], ur.at[4])
    AC.spread(uh.at[ds8(p, 8)], uh, 8, us2.at[4], ur2.at[4])
    AC.collect(uh, 8, us2.at[4], ur2.at[4])
    first = to_sibling(uh, uh, 1)
    AG.collect(W0, 32, zs.at[pl.ds(24, 8)], zr.at[pl.ds(24, 8)])
    first.wait_recv()
    u0 = mm(U0[...], W0[...], 1, 1)
    flying = {}
    def p1(it, h):
        j = 2 * it - 2 + h
        UP[j] = mm(S[...], V[2 * it - 2 + h])
        flying[j] = to_sibling(UP.at[j, half(1 - core, 128)], SB.at[j], 2 + 2 * j)
    def p2(it, h):
        j = 2 * it - 2 + h
        flying[j].wait_recv()
        HB[j] = UP[j, half(core, 128), :] + SB[j]
        AC.scatter(HB.at[j], UB.at[j], us.at[j], ur.at[j])
    def p3(it, h):
        j = 2 * it - 2 + h
        uh = U.at[j, half(core, 128)]
        uh[ds8(p, 8), :] = AC.gather_sum(HB.at[j], UB.at[j], us.at[j], ur.at[j])
        AC.spread(uh.at[ds8(p, 8)], uh, 8, us2.at[j], ur2.at[j])
    def p4(it, h):
        j = 2 * it - 2 + h
        uh = U.at[j, half(core, 128)]
        AC.collect(uh, 8, us2.at[j], ur2.at[j])
        flying[j] = to_sibling(uh, uh, 3 + 2 * j)
    def p5(it, h):
        v = 2 * it + h
        if it == 0:
            u = u0[:, 128 * h:128 * h + 128]
        else:
            if flying[v - 2] is not None:
                flying[v - 2].wait_recv()
            u = U[v - 2]
        VP[v] = mm(S[...], u, 0, 0)
        AG.scatter(VP.at[v], VB.at[v], vs.at[v], vr.at[v])
    def p6(it, h):
        v = 2 * it + h
        V[v, ds8(g, 32), :] = AG.gather_sum(VP.at[v], VB.at[v], vs.at[v], vr.at[v])
        AG.spread(V.at[v, ds8(g, 32)], V.at[v], 32, vs2.at[v], vr2.at[v])
    def p7(it, h):
        v = 2 * it + h
        AG.collect(V.at[v], 32, vs2.at[v], vr2.at[v])
    p5(0, 0); p5(0, 1); p6(0, 0); p6(0, 1); p7(0, 0)
    p1(1, 0); p2(1, 0); p3(1, 0); p4(1, 0); p7(0, 1)
    for n in range(3, 6):
        a, c = (n // 2, n % 2), ((n - 1) // 2, (n - 1) % 2)
        p1(*a); p5(*c); p2(*a); p3(*a); p6(*c); p4(*a)
        if n < 5:
            p7(*c)
    def coordinates(h):
        def cpart(q, c):
            CF[h, ds8(q, 256), :] = mm(M[ds8(q, 256), :], V[4 + h])
            return c
        lax.fori_loop(0, 4, cpart, 0)
        return to_sibling(CF.at[h, half(1 - core, 512)], CSB.at[h], 11 + h)
    def coordinates_out(h, c):
        c.wait_recv()
        CHB[h] = CF[h, half(core, 512), :] + CSB[h]
        AC.scatter(CHB.at[h], CB.at[h], cs.at[h], cr.at[h])
    mine = core * 16 + p
    flying[3].wait_recv()
    flying[3] = None
    u = jnp.concatenate([U[2], U[3]], axis=1)
    KP[...] = mm(u, u, 0, 0)
    KB[ds8(g, 8), :] = KP[ds8(mine, 8), :]
    AG.spread(KP.at[ds8(mine, 8)], KB, 8, ks, kr)
    p5(2, 1)
    AG.collect(KB, 8, ks, kr)
    acc = KB[0:8, :]
    for q in range(1, 8):
        acc = acc + KB[8 * q:8 * q + 8, :]
    kh = K.at[half(core, 128)]
    kh[ds8(p, 8), :] = acc
    AC.spread(kh.at[ds8(p, 8)], kh, 8, ks2, kr2)
    p7(2, 0)
    c0 = coordinates(0)
    p6(2, 1)
    AC.collect(kh, 8, ks2, kr2)
    swap_k = to_sibling(kh, kh, 10)
    coordinates_out(0, c0)
    swap_k.wait_recv()
    A[...] = K[...]
    chol_inv_body(A, 0, 3)
    p7(2, 1)
    c1 = coordinates(1)
    chol_inv_body(A, 3, 5)
    coordinates_out(1, c1)
    chol_inv_body(A, 5, 8)
    diag = jnp.sum(jnp.where(col == row, A[...], 0.0), axis=0, keepdims=True)
    hi = jnp.max(diag, axis=1, keepdims=True); lo = jnp.min(diag, axis=1, keepdims=True)
    state[...] = jnp.broadcast_to(jnp.where(hi < SPAN * lo, 1.0, 0.0), (8, 128))
    W = jnp.where(tri, A[...], 0.0)
    mt = mm(jnp.concatenate([V[4], V[5]], axis=1), W, 1, 1)
    SQ[0] = jnp.broadcast_to(jnp.sum(mt * mt, axis=0, keepdims=True), (8, 256))
    qsib = rcopy(SQ.at[0], SQ.at[1], qs.at[0], qr.at[0], sib)
    qsib.start()
    sent.append(qsib)
    cfs = mm(jnp.concatenate([AC.gather_sum(CHB.at[h], CB.at[h], cs.at[h], cr.at[h]) for h in range(2)], axis=1), W, 1, 1)
    qsib.wait_recv()
    SQB[ds8(p, 8), :] = SQ[0] + SQ[1]
    AC.spread(SQB.at[ds8(p, 8)], SQB, 8, qs, qr)
    AC.collect(SQB, 8, qs, qr)
    sq = SQB[0:8, :]
    for q in range(1, 16):
        sq = sq + SQB[8 * q:8 * q + 8, :]
    f = 1.0 / jnp.sqrt(sq[0:1, :] / 8192.0 + 1e-06)
    coef[...] = cfs * (f * (1.0 / math.sqrt(8192)))
    basis[...] = (mt * f).T
    drain()


def merge_all(hs, gt, idx):
    D = pltpu.SemaphoreType.DMA
    V = lambda *s: pltpu.VMEM(s, F32)
    return pl.pallas_call(
        merge_kernel,
        out_shape=[jax.ShapeDtypeStruct((32, 256), F32), jax.ShapeDtypeStruct((256, 256), F32), jax.ShapeDtypeStruct((8, 128), F32)],
        in_specs=[VM, VM, VM], out_specs=[VM, VM, VM],
        scratch_shapes=[
            V(200, 128), V(32, 200, 128), V(1024, 256), V(8, 32, 128), V(3, 32, 256), V(3, 2, 4, 4, 32, 256),
            V(256, 256), V(256, 256), V(256, 256), V(256, 256), V(256, 256), V(256, 256),
            V(256, 256), V(128, 256), V(128, 256), V(16, 8, 256), V(256, 256),
            V(4, 256, 128), V(4, 128, 128), V(4, 128, 128), V(4, 16, 8, 128), V(4, 256, 128),
            V(6, 256, 128), V(6, 8, 32, 128), V(6, 256, 128),
            V(256, 256), V(64, 256), V(256, 256),
            V(2, 1024, 128), V(2, 512, 128), V(2, 512, 128), V(2, 16, 32, 128), V(2, 8, 256), V(128, 256),
            D((80,)), D((32, 2)), D((4,)), D((3, 16)), D((3, 16)), D((16,)), D((16,)),
            D((5, 16)), D((5, 16)), D((5, 16)), D((5, 16)), D((6, 8)), D((6, 8)), D((6, 8)), D((6, 8)),
            D((8,)), D((8,)), D((16,)), D((16,)), D((2, 16)), D((2, 16)), D((16,)), D((16,)), D((32,)), D((32,)),
        ],
        compiler_params=pltpu.CompilerParams(collective_id=1, has_side_effects=True, vmem_limit_bytes=56 << 20),
    )(hs, gt, idx)


def merge_slow(hs, gt, doc_index):
    def orth(Y):
        return mm(Y, chol_inv(mm(Y, Y, 0, 0)), 1, 1)
    def sum_parts(x, axis, n):
        r = x.shape[0] // n
        return lax.all_to_all(x, axis, split_axis=0, concat_axis=0, tiled=True).reshape(n, r, x.shape[1]).sum(axis=0)
    def gather(x, axis, n):
        return lax.all_to_all(jnp.tile(x, (n, 1)), axis, split_axis=0, concat_axis=0, tiled=True)
    def total(x):
        return gather(sum_parts(x, "dev", 32), "dev", 32)
    own = (doc_index == jnp.arange(DOC_DEV, dtype=jnp.int32)[:, None]).astype(F32)
    weighted = own[:, None, :] * gt[None, :, :]
    rows = mm(weighted.reshape(-1, 128), hs).reshape(DOC_DEV, 8192) * (1.0 / math.sqrt(8192))
    block = lax.all_to_all(rows, "dev", split_axis=1, concat_axis=0, tiled=True)
    G = total(mm(block, block, 1, 1))
    Q = orth(G[:, :RANK])
    for _ in range(ITERS):
        Q = orth(mm(G, Q))
    stacked = gather(mm(Q, block, 0, 0), "group", 8)
    Q = orth(total(mm(stacked, stacked[:RANK], 1, 1)))
    for _ in range(ITERS):
        Q = orth(total(mm(stacked, mm(stacked, Q, 0, 0))))
    merged = mm(Q, stacked, 0, 0)
    squares = total(jnp.broadcast_to(jnp.sum(merged * merged, axis=1)[None, :], (32, RANK)))[0]
    basis = merged * (1.0 / jnp.sqrt(squares / 8192.0 + 1e-06))[:, None]
    summed = sum_parts(mm(block, basis, 1, 1), "dev", 32)
    return summed / math.sqrt(8192), basis


def on_device(hidden_acts, out_grads, doc_index, proj_hidden, proj_grad):
    hs = lax.dot_general(hidden_acts, proj_hidden, (((1,), (1,)), ((), ())), preferred_element_type=F32)
    gt = lax.dot_general(proj_grad, out_grads, (((1,), (1,)), ((), ())), preferred_element_type=F32)
    coef, basis, state = merge_all(hs, gt, doc_index)
    return lax.cond(state[0, 0] > 0.5, lambda: (coef, basis), lambda: merge_slow(hs, gt, doc_index))


def solution(mesh):
    return jax.shard_map(
        on_device,
        mesh=mesh,
        in_specs=(
            P(("group", "dev"), None),
            P(("group", "dev"), None),
            P(("group", "dev"), None),
            P(),
            P(),
        ),
        out_specs=(P(("group", "dev"), None), P(None, "dev")),
        check_vma=False,
    )
```

```python
import functools
import math

import jax
import jax.numpy as jnp
from jax import lax
from jax.experimental import pallas as pl
from jax.experimental.pallas import tpu as pltpu
from jax.sharding import PartitionSpec as P

RANK = 256
ITERS = 2
DOC_DEV = 32
F32 = jnp.float32
BF = jnp.bfloat16
MESH = pl.DeviceIdType.MESH
VM = pl.BlockSpec(memory_space=pltpu.VMEM)
HI = lax.Precision.HIGHEST
SPAN = 600.0


def split3(x):
    h=x.astype(BF); r=x-h.astype(F32); m=r.astype(BF); l=(r-m.astype(F32)).astype(BF)
    return h,m,l

def panel_factor(P, p, nb):
    n=P.shape[1]
    lane=lax.broadcasted_iota(jnp.int32,(nb,n),1)
    row=lax.broadcasted_iota(jnp.int32,(nb,n),0)
    rowb=lax.broadcasted_iota(jnp.int32,(nb,128),0)
    S=jnp.ones((nb,128),F32)
    for leaf in range(nb//8):
        c0=nb*p+8*leaf
        B=[jnp.broadcast_to(P[:,c0+j:c0+j+1],(nb,128)) for j in range(8)]
        for k in range(8):
            rk=8*leaf+k
            pv=B[k][rk:rk+1,:]
            rp=1.0/pv
            f=jnp.where(rowb>rk,B[k]*rp,0.0)
            for j in range(k+1,8):
                B[j]=B[j]-f*B[j][rk:rk+1,:]
            S=jnp.where(rowb==rk,lax.rsqrt(pv),S)
            hit=lane==(c0+k)
            prow=jnp.where(hit[0:1],1.0,P[rk:rk+1,:])
            ff=jnp.concatenate([f]*(n//128),axis=1)
            P=jnp.where(hit&(row>rk),0.0,jnp.where(hit&(row==rk),1.0,P))-ff*prow
    return P*jnp.concatenate([S]*(n//128),axis=1)

def chol_inv_body(A, first, last, nb=32):
    n=A.shape[0]
    for p in range(first, last):
        r0=nb*p; r1=r0+nb
        R=panel_factor(A[r0:r1,:],p,nb)
        A[r0:r1,:]=R
        if r1<n:
            plane=lax.broadcasted_iota(jnp.int32,(nb,n),1); prow=lax.broadcasted_iota(jnp.int32,(nb,n),0)
            R=jnp.where((plane>=r0)&(plane<r1)&(plane-r0>prow),0.0,R)
            h,m,l=split3(R)
            rhs=jnp.concatenate([h,m,h,l,m,h],axis=0)
            lh,lm,ll=h[:,r1:],m[:,r1:],l[:,r1:]
            lhs=jnp.concatenate([lh,lh,lm,lh,lm,ll],axis=0)
            upd=lax.dot_general(lhs,rhs,(((0,),(0,)),((),())),preferred_element_type=F32)
            lane=lax.broadcasted_iota(jnp.int32,(n-r1,n),1)
            T=A[r1:,:]
            A[r1:,:]=jnp.where((lane>=r0)&(lane<r1),0.0,T)-upd


def chol_kernel(k_ref, w_ref, A):
    A[...] = k_ref[...]
    chol_inv_body(A, 0, 8)
    r = lax.broadcasted_iota(jnp.int32, (256, 256), 0); c = lax.broadcasted_iota(jnp.int32, (256, 256), 1)
    w_ref[...] = jnp.where(c <= r, A[...], 0.0)


def chol_inv(K):
    return pl.pallas_call(
        chol_kernel, out_shape=jax.ShapeDtypeStruct((256, 256), F32), in_specs=[VM], out_specs=VM,
        scratch_shapes=[pltpu.VMEM((256, 256), F32)], compiler_params=pltpu.CompilerParams(vmem_limit_bytes=32 << 20),
    )(K)


def rcopy(src, dst, ss, rs, dev):
    return pltpu.make_async_remote_copy(src_ref=src, dst_ref=dst, send_sem=ss, recv_sem=rs, device_id=dev, device_id_type=MESH)


def mm(a, b, ca=1, cb=0):
    return lax.dot_general(a, b, (((ca,), (cb,)), ((), ())), precision=HI, preferred_element_type=F32)


def dotb(a, b, ca=1, cb=0):
    return lax.dot_general(a, b, (((ca,), (cb,)), ((), ())), preferred_element_type=F32)


def ds8(i, r):
    return pl.ds(pl.multiple_of(i * r, 8), r)


class Axis:
    def __init__(self, n, me, dev, sent):
        self.n, self.me, self.dev, self.sent = n, me, dev, sent

    def send(self, src, dst, ss, rs, q):
        c = rcopy(src, dst, ss, rs, self.dev(q))
        c.start()
        self.sent.append(c)

    def each(self, f):
        h = self.n // 2
        for k in sorted(range(1, self.n), key=lambda k: abs(k - h)):
            f(k, lax.rem(self.me + k, self.n))

    def scatter(self, src, buf, ss, rs):
        n, r = self.n, src.shape[0] // self.n
        self.each(lambda k, q: self.send(src.at[ds8(q, r)], buf.at[n - k], ss.at[k], rs.at[n - k], q))

    def gather_sum(self, src, buf, ss, rs):
        r = src.shape[0] // self.n
        acc = src[ds8(self.me, r), :]
        for k in range(1, self.n):
            rcopy(buf.at[k], buf.at[k], ss.at[k], rs.at[k], self.dev(self.me)).wait_recv()
            acc = acc + buf[k]
        return acc

    def spread(self, src, out, r, ss, rs):
        n = self.n
        self.each(lambda k, q: self.send(src, out.at[ds8(self.me, r)], ss.at[k], rs.at[n - k], q))

    def collect(self, out, r, ss, rs):
        self.each(lambda k, q: rcopy(out.at[ds8(q, r)], out.at[ds8(q, r)], ss.at[k], rs.at[k], self.dev(self.me)).wait_recv())


def ag_tokens(g, me, x_ref, out, ss, rs, ls, sent):
    core = lax.rem(me, 2); x = lax.rem(me // 2, 4); y = me // 8
    def did(yy, xx): return (g, (yy * 4 + xx) * 2 + core)
    def slot(yy, xx): return core * 16 + yy * 4 + xx
    xs = [lax.rem(x + k, 4) for k in (1, 2, 3)]; ys = [lax.rem(y + k, 4) for k in (1, 2, 3)]
    sib = (g, (y * 4 + x) * 2 + 1 - core)
    mine = slot(y, x)
    lc = pltpu.make_async_copy(x_ref, out.at[mine], ls); lc.start()
    H = [pl.ds(0, 104), pl.ds(104, 96)]
    sends = []
    def send(src, owner, h, dev):
        c = rcopy(src, out.at[owner, H[h]], ss.at[len(sends)], rs.at[owner, h], dev); c.start(); sends.append(c)
    for k in range(3):
        send(x_ref.at[H[0]], mine, 0, did(y, xs[k]))
        send(x_ref.at[H[1]], mine, 1, did(ys[k], x))
    for k in range(3):
        send(x_ref.at[H[0]], mine, 0, did(ys[k], x))
        send(x_ref.at[H[1]], mine, 1, did(y, xs[k]))
    for h in range(2): send(x_ref.at[H[h]], mine, h, sib)
    def wait(owner, h):
        rcopy(out.at[owner, H[h]], out.at[owner, H[h]], ss.at[0], rs.at[owner, h], sib).wait_recv()
    order = (0, 2, 1)
    for k in order:
        ox = slot(y, xs[k]); oy = slot(ys[k], x)
        wait(ox, 0)
        for q in range(3): send(out.at[ox, H[0]], ox, 0, did(ys[q], x))
        send(out.at[ox, H[0]], ox, 0, sib)
        wait(oy, 1)
        for q in range(3): send(out.at[oy, H[1]], oy, 1, did(y, xs[q]))
        send(out.at[oy, H[1]], oy, 1, sib)
    for k in order:
        ox = slot(y, xs[k]); oy = slot(ys[k], x)
        wait(oy, 0); send(out.at[oy, H[0]], oy, 0, sib)
        wait(ox, 1); send(out.at[ox, H[1]], ox, 1, sib)
    for k in order:
        for q in order:
            o = slot(ys[k], xs[q])
            for h in range(2):
                wait(o, h); send(out.at[o, H[h]], o, h, sib)
    lc.wait()
    sent.extend(sends)
    def other_core():
        def rest(j, c):
            for h in range(2): wait((1 - core) * 16 + j, h)
            return c
        lax.fori_loop(0, 16, rest, 0)
    return other_core


def ag_block(g, me, x_ref, out, ss, rs, ls, sent, beside=lambda i: None):
    core = lax.rem(me, 2); x = lax.rem(me // 2, 4); y = me // 8
    hr = x_ref.shape[0] // 2
    def did(yy, xx): return (g, (yy * 4 + xx) * 2 + core)
    sib = (g, (y * 4 + x) * 2 + 1 - core)
    lc = pltpu.make_async_copy(x_ref, out.at[core, y, x], ls); lc.start()
    A, B = pl.ds(0, hr), pl.ds(hr, hr)
    def send(src, dst, i, j, dev):
        c = rcopy(src, dst, ss.at[i], rs.at[j], dev); c.start(); sent.append(c)
    def wait(ref, j):
        rcopy(ref, ref, ss.at[0], rs.at[j], sib).wait_recv()
    for k in (1, 3, 2):
        send(x_ref.at[A], out.at[core, y, x, A], k, 4 - k, did(y, lax.rem(x + k, 4)))
        send(x_ref.at[B], out.at[core, y, x, B], 4 + k, 8 - k, did(lax.rem(y + k, 4), x))
    beside(0)
    lc.wait()
    for k in (1, 2, 3): wait(out.at[core, y, lax.rem(x + k, 4), A], k)
    row = out.at[core, y, :, A]
    for k in (1, 3, 2): send(row, row, 8 + k, 12 - k, did(lax.rem(y + k, 4), x))
    for k in (1, 2, 3): wait(out.at[core, lax.rem(y + k, 4), x, B], 4 + k)
    column = out.at[core, :, x, B]
    for k in (1, 3, 2): send(column, column, 12 + k, 16 - k, did(y, lax.rem(x + k, 4)))
    beside(1)
    for k in (1, 2, 3): wait(out.at[core, lax.rem(y + k, 4), :, A], 8 + k)
    send(out.at[core, :, :, A], out.at[core, :, :, A], 0, 0, sib)
    for k in (1, 2, 3): wait(out.at[core, :, lax.rem(x + k, 4), B], 12 + k)
    send(out.at[core, :, :, B], out.at[core, :, :, B], 4, 4, sib)
    beside(2)
    wait(out.at[1 - core, :, :, A], 0)
    wait(out.at[1 - core, :, :, B], 4)


def token_blocks(hs_parts, gt_cat, own3, idx, tokall, b0):
    Hs, Gc = [], []
    for s in range(4):
        Hs.append(split3(tokall[b0 + s, 0:128, :]))
        h, m, l = split3(tokall[b0 + s, 128:192, :])
        Gc.append(jnp.concatenate([h, m, h, l, m, h], axis=0))
    h, m, l = [jnp.concatenate([x[i] for x in Hs], axis=0) for i in range(3)]
    ah, am, al = hs_parts
    A = dotb(jnp.concatenate([ah, am], axis=1), jnp.concatenate([h, h], axis=1), 1, 1)
    A = A + dotb(jnp.concatenate([ah, al], axis=1), jnp.concatenate([m, h], axis=1), 1, 1)
    A = A + dotb(jnp.concatenate([ah, am], axis=1), jnp.concatenate([l, m], axis=1), 1, 1)
    B = dotb(gt_cat, jnp.concatenate(Gc, axis=1))
    th, tm, tl = split3(A * B)
    T = dotb(own3, jnp.concatenate([th, tm, tl], axis=0))
    r4 = lax.broadcasted_iota(jnp.int32, (128, 512), 0).astype(F32)
    marks = jnp.concatenate([tokall[b0 + s, 192:193, :] for s in range(4)], axis=1)
    O4 = (r4 == marks).astype(F32)
    O4b = O4.astype(BF)
    th, tm, tl = split3(T)
    G4 = dotb(th, O4b, 1, 1) + dotb(tm, O4b, 1, 1) + dotb(tl, O4b, 1, 1)
    return G4, O4, Hs


def merge_kernel(hs_in, gt_in, idx_in, coef, basis, state, tok, tokall, M, Gown, ysrc, Y, A, S, X, Z, W0, W0S, UP0, SB0, HB0, UB0, U0,
                 UP, SB, HB, UB, U, VP, VB, V, KP, KB, K, CF, CSB, CHB, CB, SQ, SQB,
                 ag_s, ag_r, ag_l, ys, yr, bs, br, us, ur, us2, ur2, vs, vr, vs2, vr2, ks, kr, ks2, kr2, cs, cr, qs, qr, zs, zr):
    g = lax.axis_index("group"); d = lax.axis_index("dev")
    core = lax.rem(d, 2); p = d // 2
    sib = (g, 2 * p + 1 - core)
    sent = []
    def drain():
        @pl.when(g == 0)
        def _():
            for k in range(1, 8):
                rcopy(Z.at[ds8(0, 32)], Z.at[ds8(0, 32)], zs.at[k], zr.at[0], (g, d)).wait_send()
                rcopy(Z.at[ds8(0, 32)], Z.at[ds8(0, 32)], zs.at[16 + k], zr.at[0], (g, d)).wait_send()
        for c in sent:
            c.wait_send()
    AC = Axis(16, p, lambda i: (g, 2 * i + core), sent)
    AG = Axis(8, g, lambda i: (i, d), sent)
    b = pltpu.get_barrier_semaphore()
    AC.each(lambda k, q: pl.semaphore_signal(b, inc=1, device_id=AC.dev(q), device_id_type=MESH))
    AG.each(lambda k, q: pl.semaphore_signal(b, inc=1, device_id=AG.dev(q), device_id_type=MESH))
    pl.semaphore_signal(b, inc=1, device_id=sib, device_id_type=MESH)
    tok[0:128, :] = hs_in[...]
    tok[128:192, :] = gt_in[...]
    idx = idx_in[0:1, :]
    tok[192:200, :] = jnp.broadcast_to(idx + 32 * lax.rem(p, 4), (8, 128)).astype(F32)
    half = lambda c, n: pl.ds(pl.multiple_of(c * n, 8), n)
    pl.semaphore_wait(b, 23)
    other_core = ag_tokens(g, d, tok, tokall, ag_s, ag_r, ag_l.at[3], sent)
    hs_parts = split3(tok[0:128, :])
    h, m, l = split3(tok[128:192, :].T)
    gt_cat = jnp.concatenate([h, h, m, h, m, l], axis=1)
    drow = lax.broadcasted_iota(jnp.int32, (32, 128), 0)
    own = (jnp.broadcast_to(idx, (32, 128)) == drow).astype(BF)
    own3 = jnp.concatenate([own, own, own], axis=1)
    par = lax.rem(d, 4)
    gbase = pl.multiple_of((d // 4) * 8, 8)
    r8 = lax.broadcasted_iota(jnp.int32, (8, 128), 0)
    def four(q, c):
        G4, O4, Hs = token_blocks(hs_parts, gt_cat, own3, idx, tokall, 4 * q)
        Gown[q] = G4 * (1.0 / 8192)
        for s in range(4):
            g8 = tokall[4 * q + s, pl.ds(128 + gbase, 8), :]
            O1 = O4[32 * s:32 * s + 32, 128 * s:128 * s + 128]
            g0 = jnp.sum(jnp.where(r8 == 2 * par, g8, 0.0), axis=0, keepdims=True)
            g1 = jnp.sum(jnp.where(r8 == 2 * par + 1, g8, 0.0), axis=0, keepdims=True)
            wh, wm, wl = split3(jnp.concatenate([O1 * g0, O1 * g1], axis=0))
            h, m, l = Hs[s]
            mr = dotb(jnp.concatenate([wh, wh, wm, wh, wm, wl], axis=1), jnp.concatenate([h, m, h, l, m, h], axis=0)) * (1.0 / math.sqrt(8192))
            M[ds8(4 * q + s, 32), 0:128] = mr[0:32]
            M[ds8(4 * q + s, 32), 128:256] = mr[32:64]
        return c
    four(4 * core, 0)
    other_core()
    four(4 - 4 * core, 0)
    def later(i):
        def two(j, c):
            return four(4 * j + i + 1, c)
        lax.fori_loop(0, 2, two, 0)
    y0, y1 = Gown[0], Gown[4]
    ysrc[0] = jnp.concatenate([(y1 if s % 2 else y0)[:, 32 * (s // 2):32 * (s // 2) + 32] for s in range(8)], axis=1)
    for it in range(3):
        ag_block(g, d, ysrc.at[it], Y.at[it], ys.at[it], yr.at[it], ag_l.at[it], sent, later if it == 0 else lambda i: None)
        if it < 2:
            acc = jnp.zeros((32, 256), F32)
            for q in range(8):
                acc = acc + mm(Gown[q], Y[it, q // 4, q % 4].reshape(128, 256))
            ysrc[it + 1] = acc
    def zpart(q, acc):
        yb = Y[2, q // 2, pl.ds(2 * lax.rem(q, 2), 2)].reshape(256, 256)
        return acc + mm(yb, M[ds8(q, 256), :], 0, 0)
    def gram(q, acc):
        yb = Y[2, q // 2, pl.ds(2 * lax.rem(q, 2), 2)].reshape(256, 256)
        return acc + mm(yb, yb, 0, 0)
    zero = jnp.zeros((256, 256), F32)
    z1 = lax.fori_loop(0, 4, zpart, zero)
    Z[...] = z1
    @pl.when(g == 0)
    def _():
        for k in range(1, 8):
            rcopy(Z.at[ds8(k, 32)], X.at[ds8(k, 32)], zs.at[k], zr.at[0], (k, d)).start()
        X[0:32, :] = Z[0:32, :]
    A[...] = lax.fori_loop(0, 4, gram, zero)
    chol_inv_body(A, 0, 3)
    @pl.when(g > 0)
    def _():
        rcopy(X.at[ds8(g, 32)], X.at[ds8(g, 32)], zs.at[0], zr.at[0], (g, d)).wait_recv()
    AG.spread(X.at[ds8(g, 32)], X, 32, zs.at[pl.ds(8, 8)], zr.at[pl.ds(8, 8)])
    chol_inv_body(A, 3, 8)
    row = lax.broadcasted_iota(jnp.int32, (256, 256), 0); col = lax.broadcasted_iota(jnp.int32, (256, 256), 1)
    tri = col <= row
    diag = jnp.sum(jnp.where(col == row, A[...], 0.0), axis=0, keepdims=True)
    hi = jnp.max(diag, axis=1, keepdims=True); lo = jnp.min(diag, axis=1, keepdims=True)
    W = jnp.where(tri, A[...], 0.0) + jnp.where(hi < SPAN * lo, 0.0, jnp.nan)
    W0S[...] = W
    @pl.when(g == 0)
    def _():
        for k in range(1, 8):
            rcopy(W0S.at[ds8(k, 32)], W0.at[ds8(k, 32)], zs.at[16 + k], zr.at[16], (k, d)).start()
        W0[0:32, :] = W0S[0:32, :]
    S[...] = mm(W, z1)
    AG.collect(X, 32, zs.at[pl.ds(8, 8)], zr.at[pl.ds(8, 8)])
    xt = X[...].T
    def to_sibling(src, dst, i):
        c = rcopy(src, dst, bs.at[i], br.at[i], sib)
        c.start()
        sent.append(c)
        return c
    UP0[...] = mm(S[...], xt)
    first = to_sibling(UP0.at[half(1 - core, 128)], SB0, 0)
    @pl.when(g > 0)
    def _():
        rcopy(W0.at[ds8(g, 32)], W0.at[ds8(g, 32)], zs.at[0], zr.at[16], (g, d)).wait_recv()
    AG.spread(W0.at[ds8(g, 32)], W0, 32, zs.at[pl.ds(24, 8)], zr.at[pl.ds(24, 8)])
    first.wait_recv()
    HB0[...] = UP0[half(core, 128), :] + SB0[...]
    AC.scatter(HB0, UB0, us.at[4], ur.at[4])
    uh = U0.at[half(core, 128)]
    uh[ds8(p, 8), :] = AC.gather_sum(HB0, UB0, us.at[4], ur.at[4])
    AC.spread(uh.at[ds8(p, 8)], uh, 8, us2.at[4], ur2.at[4])
    AC.collect(uh, 8, us2.at[4], ur2.at[4])
    first = to_sibling(uh, uh, 1)
    AG.collect(W0, 32, zs.at[pl.ds(24, 8)], zr.at[pl.ds(24, 8)])
    first.wait_recv()
    u0 = mm(U0[...], W0[...], 1, 1)
    flying = {}
    def p1(it, h):
        j = 2 * it - 2 + h
        UP[j] = mm(S[...], V[2 * it - 2 + h])
        flying[j] = to_sibling(UP.at[j, half(1 - core, 128)], SB.at[j], 2 + 2 * j)
    def p2(it, h):
        j = 2 * it - 2 + h
        flying[j].wait_recv()
        HB[j] = UP[j, half(core, 128), :] + SB[j]
        AC.scatter(HB.at[j], UB.at[j], us.at[j], ur.at[j])
    def p3(it, h):
        j = 2 * it - 2 + h
        uh = U.at[j, half(core, 128)]
        uh[ds8(p, 8), :] = AC.gather_sum(HB.at[j], UB.at[j], us.at[j], ur.at[j])
        AC.spread(uh.at[ds8(p, 8)], uh, 8, us2.at[j], ur2.at[j])
    def p4(it, h):
        j = 2 * it - 2 + h
        uh = U.at[j, half(core, 128)]
        AC.collect(uh, 8, us2.at[j], ur2.at[j])
        flying[j] = to_sibling(uh, uh, 3 + 2 * j)
    def p5(it, h):
        v = 2 * it + h
        if it == 0:
            u = u0[:, 128 * h:128 * h + 128]
        else:
            if flying[v - 2] is not None:
                flying[v - 2].wait_recv()
            u = U[v - 2]
        VP[v] = mm(S[...], u, 0, 0)
        AG.scatter(VP.at[v], VB.at[v], vs.at[v], vr.at[v])
    def p6(it, h):
        v = 2 * it + h
        V[v, ds8(g, 32), :] = AG.gather_sum(VP.at[v], VB.at[v], vs.at[v], vr.at[v])
        AG.spread(V.at[v, ds8(g, 32)], V.at[v], 32, vs2.at[v], vr2.at[v])
    def p7(it, h):
        v = 2 * it + h
        AG.collect(V.at[v], 32, vs2.at[v], vr2.at[v])
    p5(0, 0); p5(0, 1); p6(0, 0); p6(0, 1); p7(0, 0)
    p1(1, 0); p2(1, 0); p3(1, 0); p4(1, 0); p7(0, 1)
    for n in range(3, 6):
        a, c = (n // 2, n % 2), ((n - 1) // 2, (n - 1) % 2)
        p1(*a); p5(*c); p2(*a); p3(*a); p6(*c); p4(*a)
        if n < 5:
            p7(*c)
    def coordinates(h):
        def cpart(q, c):
            CF[h, ds8(q, 256), :] = mm(M[ds8(q, 256), :], V[4 + h])
            return c
        lax.fori_loop(0, 4, cpart, 0)
        return to_sibling(CF.at[h, half(1 - core, 512)], CSB.at[h], 11 + h)
    def coordinates_out(h, c):
        c.wait_recv()
        CHB[h] = CF[h, half(core, 512), :] + CSB[h]
        AC.scatter(CHB.at[h], CB.at[h], cs.at[h], cr.at[h])
    mine = core * 16 + p
    flying[3].wait_recv()
    flying[3] = None
    u = jnp.concatenate([U[2], U[3]], axis=1)
    KP[...] = mm(u, u, 0, 0)
    KB[ds8(g, 8), :] = KP[ds8(mine, 8), :]
    AG.spread(KP.at[ds8(mine, 8)], KB, 8, ks, kr)
    p5(2, 1)
    AG.collect(KB, 8, ks, kr)
    acc = KB[0:8, :]
    for q in range(1, 8):
        acc = acc + KB[8 * q:8 * q + 8, :]
    kh = K.at[half(core, 128)]
    kh[ds8(p, 8), :] = acc
    AC.spread(kh.at[ds8(p, 8)], kh, 8, ks2, kr2)
    p7(2, 0)
    c0 = coordinates(0)
    p6(2, 1)
    AC.collect(kh, 8, ks2, kr2)
    swap_k = to_sibling(kh, kh, 10)
    coordinates_out(0, c0)
    swap_k.wait_recv()
    A[...] = K[...]
    chol_inv_body(A, 0, 3)
    p7(2, 1)
    c1 = coordinates(1)
    chol_inv_body(A, 3, 5)
    coordinates_out(1, c1)
    chol_inv_body(A, 5, 8)
    diag = jnp.sum(jnp.where(col == row, A[...], 0.0), axis=0, keepdims=True)
    hi = jnp.max(diag, axis=1, keepdims=True); lo = jnp.min(diag, axis=1, keepdims=True)
    state[...] = jnp.broadcast_to(jnp.where(hi < SPAN * lo, 1.0, 0.0), (8, 128))
    W = jnp.where(tri, A[...], 0.0)
    mt = mm(jnp.concatenate([V[4], V[5]], axis=1), W, 1, 1)
    SQ[0] = jnp.broadcast_to(jnp.sum(mt * mt, axis=0, keepdims=True), (8, 256))
    qsib = rcopy(SQ.at[0], SQ.at[1], qs.at[0], qr.at[0], sib)
    qsib.start()
    sent.append(qsib)
    cfs = mm(jnp.concatenate([AC.gather_sum(CHB.at[h], CB.at[h], cs.at[h], cr.at[h]) for h in range(2)], axis=1), W, 1, 1)
    qsib.wait_recv()
    SQB[ds8(p, 8), :] = SQ[0] + SQ[1]
    AC.spread(SQB.at[ds8(p, 8)], SQB, 8, qs, qr)
    AC.collect(SQB, 8, qs, qr)
    sq = SQB[0:8, :]
    for q in range(1, 16):
        sq = sq + SQB[8 * q:8 * q + 8, :]
    f = 1.0 / jnp.sqrt(sq[0:1, :] / 8192.0 + 1e-06)
    coef[...] = cfs * (f * (1.0 / math.sqrt(8192)))
    basis[...] = (mt * f).T
    drain()


def merge_all(hs, gt, idx):
    D = pltpu.SemaphoreType.DMA
    V = lambda *s: pltpu.VMEM(s, F32)
    return pl.pallas_call(
        merge_kernel,
        out_shape=[jax.ShapeDtypeStruct((32, 256), F32), jax.ShapeDtypeStruct((256, 256), F32), jax.ShapeDtypeStruct((8, 128), F32)],
        in_specs=[VM, VM, VM], out_specs=[VM, VM, VM],
        scratch_shapes=[
            V(200, 128), V(32, 200, 128), V(1024, 256), V(8, 32, 128), V(3, 32, 256), V(3, 2, 4, 4, 32, 256),
            V(256, 256), V(256, 256), V(256, 256), V(256, 256), V(256, 256), V(256, 256),
            V(256, 256), V(128, 256), V(128, 256), V(16, 8, 256), V(256, 256),
            V(4, 256, 128), V(4, 128, 128), V(4, 128, 128), V(4, 16, 8, 128), V(4, 256, 128),
            V(6, 256, 128), V(6, 8, 32, 128), V(6, 256, 128),
            V(256, 256), V(64, 256), V(256, 256),
            V(2, 1024, 128), V(2, 512, 128), V(2, 512, 128), V(2, 16, 32, 128), V(2, 8, 256), V(128, 256),
            D((80,)), D((32, 2)), D((4,)), D((3, 16)), D((3, 16)), D((16,)), D((16,)),
            D((5, 16)), D((5, 16)), D((5, 16)), D((5, 16)), D((6, 8)), D((6, 8)), D((6, 8)), D((6, 8)),
            D((8,)), D((8,)), D((16,)), D((16,)), D((2, 16)), D((2, 16)), D((16,)), D((16,)), D((32,)), D((32,)),
        ],
        compiler_params=pltpu.CompilerParams(collective_id=1, has_side_effects=True, vmem_limit_bytes=56 << 20),
    )(hs, gt, idx)


def merge_slow(hs, gt, doc_index):
    def orth(Y):
        return mm(Y, chol_inv(mm(Y, Y, 0, 0)), 1, 1)
    def sum_parts(x, axis, n):
        r = x.shape[0] // n
        return lax.all_to_all(x, axis, split_axis=0, concat_axis=0, tiled=True).reshape(n, r, x.shape[1]).sum(axis=0)
    def gather(x, axis, n):
        return lax.all_to_all(jnp.tile(x, (n, 1)), axis, split_axis=0, concat_axis=0, tiled=True)
    def total(x):
        return gather(sum_parts(x, "dev", 32), "dev", 32)
    own = (doc_index == jnp.arange(DOC_DEV, dtype=jnp.int32)[:, None]).astype(F32)
    weighted = own[:, None, :] * gt[None, :, :]
    rows = mm(weighted.reshape(-1, 128), hs).reshape(DOC_DEV, 8192) * (1.0 / math.sqrt(8192))
    block = lax.all_to_all(rows, "dev", split_axis=1, concat_axis=0, tiled=True)
    G = total(mm(block, block, 1, 1))
    Q = lax.fori_loop(0, ITERS + 1, lambda _, Q: orth(mm(G, Q)), jnp.eye(1024, RANK, dtype=F32))
    stacked = gather(mm(Q, block, 0, 0), "group", 8)
    Q = lax.fori_loop(0, ITERS + 1, lambda _, Q: orth(total(mm(stacked, mm(stacked, Q, 0, 0)))), jnp.eye(2048, RANK, dtype=F32))
    merged = mm(Q, stacked, 0, 0)
    squares = total(jnp.broadcast_to(jnp.sum(merged * merged, axis=1)[None, :], (32, RANK)))[0]
    basis = merged * (1.0 / jnp.sqrt(squares / 8192.0 + 1e-06))[:, None]
    summed = sum_parts(mm(block, basis, 1, 1), "dev", 32)
    return summed / math.sqrt(8192), basis


def on_device(hidden_acts, out_grads, doc_index, proj_hidden, proj_grad):
    hs = lax.dot_general(hidden_acts, proj_hidden, (((1,), (1,)), ((), ())), preferred_element_type=F32)
    gt = lax.dot_general(proj_grad, out_grads, (((1,), (1,)), ((), ())), preferred_element_type=F32)
    coef, basis, state = merge_all(hs, gt, doc_index)
    return lax.cond(state[0, 0] > 0.5, lambda: (coef, basis), lambda: merge_slow(hs, gt, doc_index))


def solution(mesh):
    return jax.shard_map(
        on_device,
        mesh=mesh,
        in_specs=(
            P(("group", "dev"), None),
            P(("group", "dev"), None),
            P(("group", "dev"), None),
            P(),
            P(),
        ),
        out_specs=(P(("group", "dev"), None), P(None, "dev")),
        check_vma=False,
    )
```

```python
import functools
import math

import jax
import jax.numpy as jnp
from jax import lax
from jax.experimental import pallas as pl
from jax.experimental.pallas import tpu as pltpu
from jax.sharding import PartitionSpec as P

RANK = 256
ITERS = 2
DOC_DEV = 32
F32 = jnp.float32
BF = jnp.bfloat16
MESH = pl.DeviceIdType.MESH
VM = pl.BlockSpec(memory_space=pltpu.VMEM)
HI = lax.Precision.HIGHEST
SPAN = 600.0


def split3(x):
    h=x.astype(BF); r=x-h.astype(F32); m=r.astype(BF); l=(r-m.astype(F32)).astype(BF)
    return h,m,l

def panel_factor(P, p, nb):
    n=P.shape[1]
    lane=lax.broadcasted_iota(jnp.int32,(nb,n),1)
    row=lax.broadcasted_iota(jnp.int32,(nb,n),0)
    rowb=lax.broadcasted_iota(jnp.int32,(nb,128),0)
    S=jnp.ones((nb,128),F32)
    for leaf in range(nb//8):
        c0=nb*p+8*leaf
        B=[jnp.broadcast_to(P[:,c0+j:c0+j+1],(nb,128)) for j in range(8)]
        for k in range(8):
            rk=8*leaf+k
            pv=B[k][rk:rk+1,:]
            rp=1.0/pv
            f=jnp.where(rowb>rk,B[k]*rp,0.0)
            for j in range(k+1,8):
                B[j]=B[j]-f*B[j][rk:rk+1,:]
            S=jnp.where(rowb==rk,lax.rsqrt(pv),S)
            hit=lane==(c0+k)
            prow=jnp.where(hit[0:1],1.0,P[rk:rk+1,:])
            ff=jnp.concatenate([f]*(n//128),axis=1)
            P=jnp.where(hit&(row>rk),0.0,jnp.where(hit&(row==rk),1.0,P))-ff*prow
    return P*jnp.concatenate([S]*(n//128),axis=1)

def chol_inv_body(A, first, last, nb=32):
    n=A.shape[0]
    for p in range(first, last):
        r0=nb*p; r1=r0+nb
        R=panel_factor(A[r0:r1,:],p,nb)
        A[r0:r1,:]=R
        if r1<n:
            plane=lax.broadcasted_iota(jnp.int32,(nb,n),1); prow=lax.broadcasted_iota(jnp.int32,(nb,n),0)
            R=jnp.where((plane>=r0)&(plane<r1)&(plane-r0>prow),0.0,R)
            h,m,l=split3(R)
            rhs=jnp.concatenate([h,m,h,l,m,h],axis=0)
            lh,lm,ll=h[:,r1:],m[:,r1:],l[:,r1:]
            lhs=jnp.concatenate([lh,lh,lm,lh,lm,ll],axis=0)
            upd=lax.dot_general(lhs,rhs,(((0,),(0,)),((),())),preferred_element_type=F32)
            lane=lax.broadcasted_iota(jnp.int32,(n-r1,n),1)
            T=A[r1:,:]
            A[r1:,:]=jnp.where((lane>=r0)&(lane<r1),0.0,T)-upd


def chol_kernel(k_ref, w_ref, A):
    A[...] = k_ref[...]
    chol_inv_body(A, 0, 8)
    r = lax.broadcasted_iota(jnp.int32, (256, 256), 0); c = lax.broadcasted_iota(jnp.int32, (256, 256), 1)
    w_ref[...] = jnp.where(c <= r, A[...], 0.0)


def chol_inv(K):
    return pl.pallas_call(
        chol_kernel, out_shape=jax.ShapeDtypeStruct((256, 256), F32), in_specs=[VM], out_specs=VM,
        scratch_shapes=[pltpu.VMEM((256, 256), F32)], compiler_params=pltpu.CompilerParams(vmem_limit_bytes=32 << 20),
    )(K)


def rcopy(src, dst, ss, rs, dev):
    return pltpu.make_async_remote_copy(src_ref=src, dst_ref=dst, send_sem=ss, recv_sem=rs, device_id=dev, device_id_type=MESH)


def mm(a, b, ca=1, cb=0):
    return lax.dot_general(a, b, (((ca,), (cb,)), ((), ())), precision=HI, preferred_element_type=F32)


def dotb(a, b, ca=1, cb=0):
    return lax.dot_general(a, b, (((ca,), (cb,)), ((), ())), preferred_element_type=F32)


def ds8(i, r):
    return pl.ds(pl.multiple_of(i * r, 8), r)


class Axis:
    def __init__(self, n, me, dev, sent):
        self.n, self.me, self.dev, self.sent = n, me, dev, sent

    def send(self, src, dst, ss, rs, q):
        c = rcopy(src, dst, ss, rs, self.dev(q))
        c.start()
        self.sent.append(c)

    def each(self, f):
        h = self.n // 2
        for k in sorted(range(1, self.n), key=lambda k: abs(k - h)):
            f(k, lax.rem(self.me + k, self.n))

    def scatter(self, src, buf, ss, rs):
        n, r = self.n, src.shape[0] // self.n
        self.each(lambda k, q: self.send(src.at[ds8(q, r)], buf.at[n - k], ss.at[k], rs.at[n - k], q))

    def gather_sum(self, src, buf, ss, rs):
        r = src.shape[0] // self.n
        acc = src[ds8(self.me, r), :]
        for k in range(1, self.n):
            rcopy(buf.at[k], buf.at[k], ss.at[k], rs.at[k], self.dev(self.me)).wait_recv()
            acc = acc + buf[k]
        return acc

    def spread(self, src, out, r, ss, rs):
        n = self.n
        self.each(lambda k, q: self.send(src, out.at[ds8(self.me, r)], ss.at[k], rs.at[n - k], q))

    def collect(self, out, r, ss, rs):
        self.each(lambda k, q: rcopy(out.at[ds8(q, r)], out.at[ds8(q, r)], ss.at[k], rs.at[k], self.dev(self.me)).wait_recv())


def ag_tokens(g, me, x_ref, out, ss, rs, ls, sent):
    core = lax.rem(me, 2); x = lax.rem(me // 2, 4); y = me // 8
    def did(yy, xx): return (g, (yy * 4 + xx) * 2 + core)
    def slot(yy, xx): return core * 16 + yy * 4 + xx
    xs = [lax.rem(x + k, 4) for k in (1, 2, 3)]; ys = [lax.rem(y + k, 4) for k in (1, 2, 3)]
    sib = (g, (y * 4 + x) * 2 + 1 - core)
    mine = slot(y, x)
    lc = pltpu.make_async_copy(x_ref, out.at[mine], ls); lc.start()
    H = [pl.ds(0, 104), pl.ds(104, 96)]
    sends = []
    def send(src, owner, h, dev):
        c = rcopy(src, out.at[owner, H[h]], ss.at[len(sends)], rs.at[owner, h], dev); c.start(); sends.append(c)
    for k in range(3):
        send(x_ref.at[H[0]], mine, 0, did(y, xs[k]))
        send(x_ref.at[H[1]], mine, 1, did(ys[k], x))
    for k in range(3):
        send(x_ref.at[H[0]], mine, 0, did(ys[k], x))
        send(x_ref.at[H[1]], mine, 1, did(y, xs[k]))
    for h in range(2): send(x_ref.at[H[h]], mine, h, sib)
    def wait(owner, h):
        rcopy(out.at[owner, H[h]], out.at[owner, H[h]], ss.at[0], rs.at[owner, h], sib).wait_recv()
    order = (0, 2, 1)
    for k in order:
        ox = slot(y, xs[k]); oy = slot(ys[k], x)
        wait(ox, 0)
        for q in range(3): send(out.at[ox, H[0]], ox, 0, did(ys[q], x))
        send(out.at[ox, H[0]], ox, 0, sib)
        wait(oy, 1)
        for q in range(3): send(out.at[oy, H[1]], oy, 1, did(y, xs[q]))
        send(out.at[oy, H[1]], oy, 1, sib)
    for k in order:
        ox = slot(y, xs[k]); oy = slot(ys[k], x)
        wait(oy, 0); send(out.at[oy, H[0]], oy, 0, sib)
        wait(ox, 1); send(out.at[ox, H[1]], ox, 1, sib)
    for k in order:
        for q in order:
            o = slot(ys[k], xs[q])
            for h in range(2):
                wait(o, h); send(out.at[o, H[h]], o, h, sib)
    lc.wait()
    sent.extend(sends)
    def other_core():
        def rest(j, c):
            for h in range(2): wait((1 - core) * 16 + j, h)
            return c
        lax.fori_loop(0, 16, rest, 0)
    return other_core


def ag_block(g, me, x_ref, out, ss, rs, ls, sent, beside=lambda i: None):
    core = lax.rem(me, 2); x = lax.rem(me // 2, 4); y = me // 8
    hr = x_ref.shape[0] // 2
    def did(yy, xx): return (g, (yy * 4 + xx) * 2 + core)
    sib = (g, (y * 4 + x) * 2 + 1 - core)
    lc = pltpu.make_async_copy(x_ref, out.at[core, y, x], ls); lc.start()
    A, B = pl.ds(0, hr), pl.ds(hr, hr)
    def send(src, dst, i, j, dev):
        c = rcopy(src, dst, ss.at[i], rs.at[j], dev); c.start(); sent.append(c)
    def wait(ref, j):
        rcopy(ref, ref, ss.at[0], rs.at[j], sib).wait_recv()
    for k in (1, 3, 2):
        send(x_ref.at[A], out.at[core, y, x, A], k, 4 - k, did(y, lax.rem(x + k, 4)))
        send(x_ref.at[B], out.at[core, y, x, B], 4 + k, 8 - k, did(lax.rem(y + k, 4), x))
    beside(0)
    lc.wait()
    for k in (1, 2, 3): wait(out.at[core, y, lax.rem(x + k, 4), A], k)
    row = out.at[core, y, :, A]
    for k in (1, 3, 2): send(row, row, 8 + k, 12 - k, did(lax.rem(y + k, 4), x))
    for k in (1, 2, 3): wait(out.at[core, lax.rem(y + k, 4), x, B], 4 + k)
    column = out.at[core, :, x, B]
    for k in (1, 3, 2): send(column, column, 12 + k, 16 - k, did(y, lax.rem(x + k, 4)))
    beside(1)
    for k in (1, 2, 3): wait(out.at[core, lax.rem(y + k, 4), :, A], 8 + k)
    send(out.at[core, :, :, A], out.at[core, :, :, A], 0, 0, sib)
    for k in (1, 2, 3): wait(out.at[core, :, lax.rem(x + k, 4), B], 12 + k)
    send(out.at[core, :, :, B], out.at[core, :, :, B], 4, 4, sib)
    beside(2)
    wait(out.at[1 - core, :, :, A], 0)
    wait(out.at[1 - core, :, :, B], 4)


def token_blocks(hs_parts, gt_cat, own3, idx, tokall, b0):
    Hs, Gc = [], []
    for s in range(4):
        Hs.append(split3(tokall[b0 + s, 0:128, :]))
        h, m, l = split3(tokall[b0 + s, 128:192, :])
        Gc.append(jnp.concatenate([h, m, h, l, m, h], axis=0))
    h, m, l = [jnp.concatenate([x[i] for x in Hs], axis=0) for i in range(3)]
    ah, am, al = hs_parts
    A = dotb(jnp.concatenate([ah, am], axis=1), jnp.concatenate([h, h], axis=1), 1, 1)
    A = A + dotb(jnp.concatenate([ah, al], axis=1), jnp.concatenate([m, h], axis=1), 1, 1)
    A = A + dotb(jnp.concatenate([ah, am], axis=1), jnp.concatenate([l, m], axis=1), 1, 1)
    B = dotb(gt_cat, jnp.concatenate(Gc, axis=1))
    th, tm, tl = split3(A * B)
    T = dotb(own3, jnp.concatenate([th, tm, tl], axis=0))
    r4 = lax.broadcasted_iota(jnp.int32, (128, 512), 0).astype(F32)
    marks = jnp.concatenate([tokall[b0 + s, 192:193, :] for s in range(4)], axis=1)
    O4 = (r4 == marks).astype(F32)
    O4b = O4.astype(BF)
    th, tm, tl = split3(T)
    G4 = dotb(th, O4b, 1, 1) + dotb(tm, O4b, 1, 1) + dotb(tl, O4b, 1, 1)
    return G4, O4, Hs


def merge_kernel(hs_in, gt_in, idx_in, coef, basis, state, tok, tokall, M, Gown, ysrc, Y, A, S, X, Z, W0, W0S, UP0, SB0, HB0, UB0, U0,
                 UP, SB, HB, UB, U, VP, VB, V, KP, KB, K, CF, CSB, CHB, CB, SQ, SQB,
                 ag_s, ag_r, ag_l, ys, yr, bs, br, us, ur, us2, ur2, vs, vr, vs2, vr2, ks, kr, ks2, kr2, cs, cr, qs, qr, zs, zr):
    g = lax.axis_index("group"); d = lax.axis_index("dev")
    core = lax.rem(d, 2); p = d // 2
    sib = (g, 2 * p + 1 - core)
    sent = []
    def drain():
        @pl.when(g == 0)
        def _():
            for k in range(1, 8):
                rcopy(Z.at[ds8(0, 32)], Z.at[ds8(0, 32)], zs.at[k], zr.at[0], (g, d)).wait_send()
                rcopy(Z.at[ds8(0, 32)], Z.at[ds8(0, 32)], zs.at[16 + k], zr.at[0], (g, d)).wait_send()
        for c in sent:
            c.wait_send()
    AC = Axis(16, p, lambda i: (g, 2 * i + core), sent)
    AG = Axis(8, g, lambda i: (i, d), sent)
    b = pltpu.get_barrier_semaphore()
    AC.each(lambda k, q: pl.semaphore_signal(b, inc=1, device_id=AC.dev(q), device_id_type=MESH))
    AG.each(lambda k, q: pl.semaphore_signal(b, inc=1, device_id=AG.dev(q), device_id_type=MESH))
    pl.semaphore_signal(b, inc=1, device_id=sib, device_id_type=MESH)
    tok[0:128, :] = hs_in[...]
    tok[128:192, :] = gt_in[...]
    idx = idx_in[0:1, :]
    tok[192:200, :] = jnp.broadcast_to(idx + 32 * lax.rem(p, 4), (8, 128)).astype(F32)
    half = lambda c, n: pl.ds(pl.multiple_of(c * n, 8), n)
    pl.semaphore_wait(b, 23)
    other_core = ag_tokens(g, d, tok, tokall, ag_s, ag_r, ag_l.at[3], sent)
    hs_parts = split3(tok[0:128, :])
    h, m, l = split3(tok[128:192, :].T)
    gt_cat = jnp.concatenate([h, h, m, h, m, l], axis=1)
    drow = lax.broadcasted_iota(jnp.int32, (32, 128), 0)
    own = (jnp.broadcast_to(idx, (32, 128)) == drow).astype(BF)
    own3 = jnp.concatenate([own, own, own], axis=1)
    par = lax.rem(d, 4)
    gbase = pl.multiple_of((d // 4) * 8, 8)
    r8 = lax.broadcasted_iota(jnp.int32, (8, 128), 0)
    def four(q, c):
        G4, O4, Hs = token_blocks(hs_parts, gt_cat, own3, idx, tokall, 4 * q)
        Gown[q] = G4 * (1.0 / 8192)
        for s in range(4):
            g8 = tokall[4 * q + s, pl.ds(128 + gbase, 8), :]
            O1 = O4[32 * s:32 * s + 32, 128 * s:128 * s + 128]
            g0 = jnp.sum(jnp.where(r8 == 2 * par, g8, 0.0), axis=0, keepdims=True)
            g1 = jnp.sum(jnp.where(r8 == 2 * par + 1, g8, 0.0), axis=0, keepdims=True)
            wh, wm, wl = split3(jnp.concatenate([O1 * g0, O1 * g1], axis=0))
            h, m, l = Hs[s]
            mr = dotb(jnp.concatenate([wh, wh, wm, wh, wm, wl], axis=1), jnp.concatenate([h, m, h, l, m, h], axis=0)) * (1.0 / math.sqrt(8192))
            M[ds8(4 * q + s, 32), 0:128] = mr[0:32]
            M[ds8(4 * q + s, 32), 128:256] = mr[32:64]
        return c
    four(4 * core, 0)
    other_core()
    four(4 - 4 * core, 0)
    def later(i):
        def two(j, c):
            return four(4 * j + i + 1, c)
        lax.fori_loop(0, 2, two, 0)
    y0, y1 = Gown[0], Gown[4]
    ysrc[0] = jnp.concatenate([(y1 if s % 2 else y0)[:, 32 * (s // 2):32 * (s // 2) + 32] for s in range(8)], axis=1)
    for it in range(3):
        ag_block(g, d, ysrc.at[it], Y.at[it], ys.at[it], yr.at[it], ag_l.at[it], sent, later if it == 0 else lambda i: None)
        if it < 2:
            acc = jnp.zeros((32, 256), F32)
            for q in range(8):
                acc = acc + mm(Gown[q], Y[it, q // 4, q % 4].reshape(128, 256))
            ysrc[it + 1] = acc
    def zpart(q, acc):
        yb = Y[2, q // 2, pl.ds(2 * lax.rem(q, 2), 2)].reshape(256, 256)
        return acc + mm(yb, M[ds8(q, 256), :], 0, 0)
    def gram(q, acc):
        yb = Y[2, q // 2, pl.ds(2 * lax.rem(q, 2), 2)].reshape(256, 256)
        return acc + mm(yb, yb, 0, 0)
    zero = jnp.zeros((256, 256), F32)
    z1 = lax.fori_loop(0, 4, zpart, zero)
    Z[...] = z1
    @pl.when(g == 0)
    def _():
        for k in range(1, 8):
            rcopy(Z.at[ds8(k, 32)], X.at[ds8(k, 32)], zs.at[k], zr.at[0], (k, d)).start()
        X[0:32, :] = Z[0:32, :]
    A[...] = lax.fori_loop(0, 4, gram, zero)
    chol_inv_body(A, 0, 3)
    @pl.when(g > 0)
    def _():
        rcopy(X.at[ds8(g, 32)], X.at[ds8(g, 32)], zs.at[0], zr.at[0], (g, d)).wait_recv()
    AG.spread(X.at[ds8(g, 32)], X, 32, zs.at[pl.ds(8, 8)], zr.at[pl.ds(8, 8)])
    chol_inv_body(A, 3, 8)
    row = lax.broadcasted_iota(jnp.int32, (256, 256), 0); col = lax.broadcasted_iota(jnp.int32, (256, 256), 1)
    tri = col <= row
    diag = jnp.sum(jnp.where(col == row, A[...], 0.0), axis=0, keepdims=True)
    hi = jnp.max(diag, axis=1, keepdims=True); lo = jnp.min(diag, axis=1, keepdims=True)
    W = jnp.where(tri, A[...], 0.0) + jnp.where(hi < SPAN * lo, 0.0, jnp.nan)
    W0S[...] = W
    @pl.when(g == 0)
    def _():
        for k in range(1, 8):
            rcopy(W0S.at[ds8(k, 32)], W0.at[ds8(k, 32)], zs.at[16 + k], zr.at[16], (k, d)).start()
        W0[0:32, :] = W0S[0:32, :]
    S[...] = mm(W, z1)
    AG.collect(X, 32, zs.at[pl.ds(8, 8)], zr.at[pl.ds(8, 8)])
    xt = X[...].T
    def to_sibling(src, dst, i):
        c = rcopy(src, dst, bs.at[i], br.at[i], sib)
        c.start()
        sent.append(c)
        return c
    UP0[...] = mm(S[...], xt)
    first = to_sibling(UP0.at[half(1 - core, 128)], SB0, 0)
    @pl.when(g > 0)
    def _():
        rcopy(W0.at[ds8(g, 32)], W0.at[ds8(g, 32)], zs.at[0], zr.at[16], (g, d)).wait_recv()
    AG.spread(W0.at[ds8(g, 32)], W0, 32, zs.at[pl.ds(24, 8)], zr.at[pl.ds(24, 8)])
    first.wait_recv()
    HB0[...] = UP0[half(core, 128), :] + SB0[...]
    AC.scatter(HB0, UB0, us.at[4], ur.at[4])
    uh = U0.at[half(core, 128)]
    uh[ds8(p, 8), :] = AC.gather_sum(HB0, UB0, us.at[4], ur.at[4])
    AC.spread(uh.at[ds8(p, 8)], uh, 8, us2.at[4], ur2.at[4])
    AC.collect(uh, 8, us2.at[4], ur2.at[4])
    first = to_sibling(uh, uh, 1)
    AG.collect(W0, 32, zs.at[pl.ds(24, 8)], zr.at[pl.ds(24, 8)])
    first.wait_recv()
    u0 = mm(U0[...], W0[...], 1, 1)
    flying = {}
    def p1(it, h):
        j = 2 * it - 2 + h
        UP[j] = mm(S[...], V[2 * it - 2 + h])
        flying[j] = to_sibling(UP.at[j, half(1 - core, 128)], SB.at[j], 2 + 2 * j)
    def p2(it, h):
        j = 2 * it - 2 + h
        flying[j].wait_recv()
        HB[j] = UP[j, half(core, 128), :] + SB[j]
        AC.scatter(HB.at[j], UB.at[j], us.at[j], ur.at[j])
    def p3(it, h):
        j = 2 * it - 2 + h
        uh = U.at[j, half(core, 128)]
        uh[ds8(p, 8), :] = AC.gather_sum(HB.at[j], UB.at[j], us.at[j], ur.at[j])
        AC.spread(uh.at[ds8(p, 8)], uh, 8, us2.at[j], ur2.at[j])
    def p4(it, h):
        j = 2 * it - 2 + h
        uh = U.at[j, half(core, 128)]
        AC.collect(uh, 8, us2.at[j], ur2.at[j])
        flying[j] = to_sibling(uh, uh, 3 + 2 * j)
    def p5(it, h):
        v = 2 * it + h
        if it == 0:
            u = u0[:, 128 * h:128 * h + 128]
        else:
            if flying[v - 2] is not None:
                flying[v - 2].wait_recv()
            u = U[v - 2]
        VP[v] = mm(S[...], u, 0, 0)
        AG.scatter(VP.at[v], VB.at[v], vs.at[v], vr.at[v])
    def p6(it, h):
        v = 2 * it + h
        V[v, ds8(g, 32), :] = AG.gather_sum(VP.at[v], VB.at[v], vs.at[v], vr.at[v])
        AG.spread(V.at[v, ds8(g, 32)], V.at[v], 32, vs2.at[v], vr2.at[v])
    def p7(it, h):
        v = 2 * it + h
        AG.collect(V.at[v], 32, vs2.at[v], vr2.at[v])
    p5(0, 0); p5(0, 1); p6(0, 0); p6(0, 1); p7(0, 0)
    p1(1, 0); p2(1, 0); p3(1, 0); p4(1, 0); p7(0, 1)
    for n in range(3, 6):
        a, c = (n // 2, n % 2), ((n - 1) // 2, (n - 1) % 2)
        p1(*a); p5(*c); p2(*a); p3(*a); p6(*c); p4(*a)
        if n < 5:
            p7(*c)
    def coordinates(h):
        def cpart(q, c):
            CF[h, ds8(q, 256), :] = mm(M[ds8(q, 256), :], V[4 + h])
            return c
        lax.fori_loop(0, 4, cpart, 0)
        return to_sibling(CF.at[h, half(1 - core, 512)], CSB.at[h], 11 + h)
    def coordinates_out(h, c):
        c.wait_recv()
        CHB[h] = CF[h, half(core, 512), :] + CSB[h]
        AC.scatter(CHB.at[h], CB.at[h], cs.at[h], cr.at[h])
    mine = core * 16 + p
    flying[3].wait_recv()
    flying[3] = None
    u = jnp.concatenate([U[2], U[3]], axis=1)
    KP[...] = mm(u, u, 0, 0)
    KB[ds8(g, 8), :] = KP[ds8(mine, 8), :]
    AG.spread(KP.at[ds8(mine, 8)], KB, 8, ks, kr)
    p5(2, 1)
    AG.collect(KB, 8, ks, kr)
    acc = KB[0:8, :]
    for q in range(1, 8):
        acc = acc + KB[8 * q:8 * q + 8, :]
    kh = K.at[half(core, 128)]
    kh[ds8(p, 8), :] = acc
    AC.spread(kh.at[ds8(p, 8)], kh, 8, ks2, kr2)
    p7(2, 0)
    c0 = coordinates(0)
    p6(2, 1)
    AC.collect(kh, 8, ks2, kr2)
    swap_k = to_sibling(kh, kh, 10)
    coordinates_out(0, c0)
    swap_k.wait_recv()
    A[...] = K[...]
    chol_inv_body(A, 0, 3)
    p7(2, 1)
    c1 = coordinates(1)
    chol_inv_body(A, 3, 5)
    coordinates_out(1, c1)
    chol_inv_body(A, 5, 8)
    diag = jnp.sum(jnp.where(col == row, A[...], 0.0), axis=0, keepdims=True)
    hi = jnp.max(diag, axis=1, keepdims=True); lo = jnp.min(diag, axis=1, keepdims=True)
    state[0, 0] = jnp.max(jnp.where(hi < SPAN * lo, 1.0, 0.0))
    W = jnp.where(tri, A[...], 0.0)
    mt = mm(jnp.concatenate([V[4], V[5]], axis=1), W, 1, 1)
    SQ[0] = jnp.broadcast_to(jnp.sum(mt * mt, axis=0, keepdims=True), (8, 256))
    qsib = rcopy(SQ.at[0], SQ.at[1], qs.at[0], qr.at[0], sib)
    qsib.start()
    sent.append(qsib)
    cfs = mm(jnp.concatenate([AC.gather_sum(CHB.at[h], CB.at[h], cs.at[h], cr.at[h]) for h in range(2)], axis=1), W, 1, 1)
    qsib.wait_recv()
    SQB[ds8(p, 8), :] = SQ[0] + SQ[1]
    AC.spread(SQB.at[ds8(p, 8)], SQB, 8, qs, qr)
    AC.collect(SQB, 8, qs, qr)
    sq = SQB[0:8, :]
    for q in range(1, 16):
        sq = sq + SQB[8 * q:8 * q + 8, :]
    f = 1.0 / jnp.sqrt(sq[0:1, :] / 8192.0 + 1e-06)
    coef[...] = cfs * (f * (1.0 / math.sqrt(8192)))
    basis[...] = (mt * f).T
    drain()


def merge_all(hs, gt, idx):
    D = pltpu.SemaphoreType.DMA
    V = lambda *s: pltpu.VMEM(s, F32)
    return pl.pallas_call(
        merge_kernel,
        out_shape=[jax.ShapeDtypeStruct((32, 256), F32), jax.ShapeDtypeStruct((256, 256), F32), jax.ShapeDtypeStruct((1, 1), F32)],
        in_specs=[VM, VM, VM], out_specs=[VM, VM, pl.BlockSpec(memory_space=pltpu.SMEM)],
        scratch_shapes=[
            V(200, 128), V(32, 200, 128), V(1024, 256), V(8, 32, 128), V(3, 32, 256), V(3, 2, 4, 4, 32, 256),
            V(256, 256), V(256, 256), V(256, 256), V(256, 256), V(256, 256), V(256, 256),
            V(256, 256), V(128, 256), V(128, 256), V(16, 8, 256), V(256, 256),
            V(4, 256, 128), V(4, 128, 128), V(4, 128, 128), V(4, 16, 8, 128), V(4, 256, 128),
            V(6, 256, 128), V(6, 8, 32, 128), V(6, 256, 128),
            V(256, 256), V(64, 256), V(256, 256),
            V(2, 1024, 128), V(2, 512, 128), V(2, 512, 128), V(2, 16, 32, 128), V(2, 8, 256), V(128, 256),
            D((80,)), D((32, 2)), D((4,)), D((3, 16)), D((3, 16)), D((16,)), D((16,)),
            D((5, 16)), D((5, 16)), D((5, 16)), D((5, 16)), D((6, 8)), D((6, 8)), D((6, 8)), D((6, 8)),
            D((8,)), D((8,)), D((16,)), D((16,)), D((2, 16)), D((2, 16)), D((16,)), D((16,)), D((32,)), D((32,)),
        ],
        compiler_params=pltpu.CompilerParams(collective_id=1, has_side_effects=True, vmem_limit_bytes=56 << 20),
    )(hs, gt, idx)


def merge_slow(hs, gt, doc_index):
    def orth(Y):
        return mm(Y, chol_inv(mm(Y, Y, 0, 0)), 1, 1)
    def sum_parts(x, axis, n):
        r = x.shape[0] // n
        return lax.all_to_all(x, axis, split_axis=0, concat_axis=0, tiled=True).reshape(n, r, x.shape[1]).sum(axis=0)
    def gather(x, axis, n):
        return lax.all_to_all(jnp.tile(x, (n, 1)), axis, split_axis=0, concat_axis=0, tiled=True)
    def total(x):
        return gather(sum_parts(x, "dev", 32), "dev", 32)
    own = (doc_index == jnp.arange(DOC_DEV, dtype=jnp.int32)[:, None]).astype(F32)
    weighted = own[:, None, :] * gt[None, :, :]
    rows = mm(weighted.reshape(-1, 128), hs).reshape(DOC_DEV, 8192) * (1.0 / math.sqrt(8192))
    block = lax.all_to_all(rows, "dev", split_axis=1, concat_axis=0, tiled=True)
    G = total(mm(block, block, 1, 1))
    Q = lax.fori_loop(0, ITERS + 1, lambda _, Q: orth(mm(G, Q)), jnp.eye(1024, RANK, dtype=F32))
    stacked = gather(mm(Q, block, 0, 0), "group", 8)
    Q = lax.fori_loop(0, ITERS + 1, lambda _, Q: orth(total(mm(stacked, mm(stacked, Q, 0, 0)))), jnp.eye(2048, RANK, dtype=F32))
    merged = mm(Q, stacked, 0, 0)
    squares = total(jnp.broadcast_to(jnp.sum(merged * merged, axis=1)[None, :], (32, RANK)))[0]
    basis = merged * (1.0 / jnp.sqrt(squares / 8192.0 + 1e-06))[:, None]
    summed = sum_parts(mm(block, basis, 1, 1), "dev", 32)
    return summed / math.sqrt(8192), basis


def on_device(hidden_acts, out_grads, doc_index, proj_hidden, proj_grad):
    hs = lax.dot_general(hidden_acts, proj_hidden, (((1,), (1,)), ((), ())), preferred_element_type=F32)
    gt = lax.dot_general(proj_grad, out_grads, (((1,), (1,)), ((), ())), preferred_element_type=F32)
    coef, basis, state = merge_all(hs, gt, doc_index)
    return lax.cond(state[0, 0] > 0.5, lambda: (coef, basis), lambda: merge_slow(hs, gt, doc_index))


def solution(mesh):
    return jax.shard_map(
        on_device,
        mesh=mesh,
        in_specs=(
            P(("group", "dev"), None),
            P(("group", "dev"), None),
            P(("group", "dev"), None),
            P(),
            P(),
        ),
        out_specs=(P(("group", "dev"), None), P(None, "dev")),
        check_vma=False,
    )
```

```python
import functools
import math

import jax
import jax.numpy as jnp
from jax import lax
from jax.experimental import pallas as pl
from jax.experimental.pallas import tpu as pltpu
from jax.sharding import PartitionSpec as P

RANK = 256
ITERS = 2
DOC_DEV = 32
F32 = jnp.float32
BF = jnp.bfloat16
MESH = pl.DeviceIdType.MESH
VM = pl.BlockSpec(memory_space=pltpu.VMEM)
HI = lax.Precision.HIGHEST
SPAN = 600.0


def split3(x):
    h=x.astype(BF); r=x-h.astype(F32); m=r.astype(BF); l=(r-m.astype(F32)).astype(BF)
    return h,m,l

def panel_factor(P, p, nb):
    n=P.shape[1]
    lane=lax.broadcasted_iota(jnp.int32,(nb,n),1)
    row=lax.broadcasted_iota(jnp.int32,(nb,n),0)
    rowb=lax.broadcasted_iota(jnp.int32,(nb,128),0)
    S=jnp.ones((nb,128),F32)
    for leaf in range(nb//8):
        c0=nb*p+8*leaf
        B=[jnp.broadcast_to(P[:,c0+j:c0+j+1],(nb,128)) for j in range(8)]
        for k in range(8):
            rk=8*leaf+k
            pv=B[k][rk:rk+1,:]
            rp=1.0/pv
            f=jnp.where(rowb>rk,B[k]*rp,0.0)
            for j in range(k+1,8):
                B[j]=B[j]-f*B[j][rk:rk+1,:]
            S=jnp.where(rowb==rk,lax.rsqrt(pv),S)
            hit=lane==(c0+k)
            prow=jnp.where(hit[0:1],1.0,P[rk:rk+1,:])
            ff=jnp.concatenate([f]*(n//128),axis=1)
            P=jnp.where(hit&(row>rk),0.0,jnp.where(hit&(row==rk),1.0,P))-ff*prow
    return P*jnp.concatenate([S]*(n//128),axis=1)

def chol_inv_body(A, first, last, nb=32):
    n=A.shape[0]
    for p in range(first, last):
        r0=nb*p; r1=r0+nb
        R=panel_factor(A[r0:r1,:],p,nb)
        A[r0:r1,:]=R
        if r1<n:
            plane=lax.broadcasted_iota(jnp.int32,(nb,n),1); prow=lax.broadcasted_iota(jnp.int32,(nb,n),0)
            R=jnp.where((plane>=r0)&(plane<r1)&(plane-r0>prow),0.0,R)
            h,m,l=split3(R)
            rhs=jnp.concatenate([h,m,h,l,m,h],axis=0)
            lh,lm,ll=h[:,r1:],m[:,r1:],l[:,r1:]
            lhs=jnp.concatenate([lh,lh,lm,lh,lm,ll],axis=0)
            upd=lax.dot_general(lhs,rhs,(((0,),(0,)),((),())),preferred_element_type=F32)
            lane=lax.broadcasted_iota(jnp.int32,(n-r1,n),1)
            T=A[r1:,:]
            A[r1:,:]=jnp.where((lane>=r0)&(lane<r1),0.0,T)-upd


def chol_kernel(k_ref, w_ref, A):
    A[...] = k_ref[...]
    chol_inv_body(A, 0, 8)
    r = lax.broadcasted_iota(jnp.int32, (256, 256), 0); c = lax.broadcasted_iota(jnp.int32, (256, 256), 1)
    w_ref[...] = jnp.where(c <= r, A[...], 0.0)


def chol_inv(K):
    return pl.pallas_call(
        chol_kernel, out_shape=jax.ShapeDtypeStruct((256, 256), F32), in_specs=[VM], out_specs=VM,
        scratch_shapes=[pltpu.VMEM((256, 256), F32)], compiler_params=pltpu.CompilerParams(vmem_limit_bytes=32 << 20),
    )(K)


def rcopy(src, dst, ss, rs, dev):
    return pltpu.make_async_remote_copy(src_ref=src, dst_ref=dst, send_sem=ss, recv_sem=rs, device_id=dev, device_id_type=MESH)


def mm(a, b, ca=1, cb=0):
    return lax.dot_general(a, b, (((ca,), (cb,)), ((), ())), precision=HI, preferred_element_type=F32)


def dotb(a, b, ca=1, cb=0):
    return lax.dot_general(a, b, (((ca,), (cb,)), ((), ())), preferred_element_type=F32)


def ds8(i, r):
    return pl.ds(pl.multiple_of(i * r, 8), r)


class Axis:
    def __init__(self, n, me, dev, sent):
        self.n, self.me, self.dev, self.sent = n, me, dev, sent

    def send(self, src, dst, ss, rs, q):
        c = rcopy(src, dst, ss, rs, self.dev(q))
        c.start()
        self.sent.append(c)

    def each(self, f):
        h = self.n // 2
        for k in sorted(range(1, self.n), key=lambda k: abs(k - h)):
            f(k, lax.rem(self.me + k, self.n))

    def scatter(self, src, buf, ss, rs):
        n, r = self.n, src.shape[0] // self.n
        self.each(lambda k, q: self.send(src.at[ds8(q, r)], buf.at[n - k], ss.at[k], rs.at[n - k], q))

    def gather_sum(self, src, buf, ss, rs):
        r = src.shape[0] // self.n
        acc = src[ds8(self.me, r), :]
        for k in range(1, self.n):
            rcopy(buf.at[k], buf.at[k], ss.at[k], rs.at[k], self.dev(self.me)).wait_recv()
            acc = acc + buf[k]
        return acc

    def spread(self, src, out, r, ss, rs):
        n = self.n
        self.each(lambda k, q: self.send(src, out.at[ds8(self.me, r)], ss.at[k], rs.at[n - k], q))

    def collect(self, out, r, ss, rs):
        self.each(lambda k, q: rcopy(out.at[ds8(q, r)], out.at[ds8(q, r)], ss.at[k], rs.at[k], self.dev(self.me)).wait_recv())


def ag_tokens(g, me, x_ref, out, ss, rs, ls, sent):
    core = lax.rem(me, 2); x = lax.rem(me // 2, 4); y = me // 8
    def did(yy, xx): return (g, (yy * 4 + xx) * 2 + core)
    def slot(yy, xx): return core * 16 + yy * 4 + xx
    xs = [lax.rem(x + k, 4) for k in (1, 2, 3)]; ys = [lax.rem(y + k, 4) for k in (1, 2, 3)]
    sib = (g, (y * 4 + x) * 2 + 1 - core)
    mine = slot(y, x)
    lc = pltpu.make_async_copy(x_ref, out.at[mine], ls); lc.start()
    H = [pl.ds(0, 104), pl.ds(104, 96)]
    sends = []
    def send(src, owner, h, dev):
        c = rcopy(src, out.at[owner, H[h]], ss.at[len(sends)], rs.at[owner, h], dev); c.start(); sends.append(c)
    for k in range(3):
        send(x_ref.at[H[0]], mine, 0, did(y, xs[k]))
        send(x_ref.at[H[1]], mine, 1, did(ys[k], x))
    for k in range(3):
        send(x_ref.at[H[0]], mine, 0, did(ys[k], x))
        send(x_ref.at[H[1]], mine, 1, did(y, xs[k]))
    for h in range(2): send(x_ref.at[H[h]], mine, h, sib)
    def wait(owner, h):
        rcopy(out.at[owner, H[h]], out.at[owner, H[h]], ss.at[0], rs.at[owner, h], sib).wait_recv()
    order = (0, 2, 1)
    for k in order:
        ox = slot(y, xs[k]); oy = slot(ys[k], x)
        wait(ox, 0)
        for q in range(3): send(out.at[ox, H[0]], ox, 0, did(ys[q], x))
        send(out.at[ox, H[0]], ox, 0, sib)
        wait(oy, 1)
        for q in range(3): send(out.at[oy, H[1]], oy, 1, did(y, xs[q]))
        send(out.at[oy, H[1]], oy, 1, sib)
    for k in order:
        ox = slot(y, xs[k]); oy = slot(ys[k], x)
        wait(oy, 0); send(out.at[oy, H[0]], oy, 0, sib)
        wait(ox, 1); send(out.at[ox, H[1]], ox, 1, sib)
    for k in order:
        for q in order:
            o = slot(ys[k], xs[q])
            for h in range(2):
                wait(o, h); send(out.at[o, H[h]], o, h, sib)
    lc.wait()
    sent.extend(sends)
    def other_core():
        def rest(j, c):
            for h in range(2): wait((1 - core) * 16 + j, h)
            return c
        lax.fori_loop(0, 16, rest, 0)
    return other_core


def ag_block(g, me, x_ref, out, ss, rs, ls, sent, beside=lambda i: None):
    core = lax.rem(me, 2); x = lax.rem(me // 2, 4); y = me // 8
    hr = x_ref.shape[0] // 2
    def did(yy, xx): return (g, (yy * 4 + xx) * 2 + core)
    sib = (g, (y * 4 + x) * 2 + 1 - core)
    lc = pltpu.make_async_copy(x_ref, out.at[core, y, x], ls); lc.start()
    A, B = pl.ds(0, hr), pl.ds(hr, hr)
    def send(src, dst, i, j, dev):
        c = rcopy(src, dst, ss.at[i], rs.at[j], dev); c.start(); sent.append(c)
    def wait(ref, j):
        rcopy(ref, ref, ss.at[0], rs.at[j], sib).wait_recv()
    for k in (1, 3, 2):
        send(x_ref.at[A], out.at[core, y, x, A], k, 4 - k, did(y, lax.rem(x + k, 4)))
        send(x_ref.at[B], out.at[core, y, x, B], 4 + k, 8 - k, did(lax.rem(y + k, 4), x))
    beside(0)
    lc.wait()
    for k in (1, 2, 3): wait(out.at[core, y, lax.rem(x + k, 4), A], k)
    row = out.at[core, y, :, A]
    for k in (1, 3, 2): send(row, row, 8 + k, 12 - k, did(lax.rem(y + k, 4), x))
    for k in (1, 2, 3): wait(out.at[core, lax.rem(y + k, 4), x, B], 4 + k)
    column = out.at[core, :, x, B]
    for k in (1, 3, 2): send(column, column, 12 + k, 16 - k, did(y, lax.rem(x + k, 4)))
    beside(1)
    for k in (1, 2, 3): wait(out.at[core, lax.rem(y + k, 4), :, A], 8 + k)
    send(out.at[core, :, :, A], out.at[core, :, :, A], 0, 0, sib)
    for k in (1, 2, 3): wait(out.at[core, :, lax.rem(x + k, 4), B], 12 + k)
    send(out.at[core, :, :, B], out.at[core, :, :, B], 4, 4, sib)
    beside(2)
    wait(out.at[1 - core, :, :, A], 0)
    wait(out.at[1 - core, :, :, B], 4)


def token_blocks(hs_parts, gt_cat, own3, idx, tokall, b0):
    Hs, Gc = [], []
    for s in range(4):
        Hs.append(split3(tokall[b0 + s, 0:128, :]))
        h, m, l = split3(tokall[b0 + s, 128:192, :])
        Gc.append(jnp.concatenate([h, m, h, l, m, h], axis=0))
    h, m, l = [jnp.concatenate([x[i] for x in Hs], axis=0) for i in range(3)]
    ah, am, al = hs_parts
    A = dotb(jnp.concatenate([ah, am], axis=1), jnp.concatenate([h, h], axis=1), 1, 1)
    A = A + dotb(jnp.concatenate([ah, al], axis=1), jnp.concatenate([m, h], axis=1), 1, 1)
    A = A + dotb(jnp.concatenate([ah, am], axis=1), jnp.concatenate([l, m], axis=1), 1, 1)
    B = dotb(gt_cat, jnp.concatenate(Gc, axis=1))
    th, tm, tl = split3(A * B)
    T = dotb(own3, jnp.concatenate([th, tm, tl], axis=0))
    r4 = lax.broadcasted_iota(jnp.int32, (128, 512), 0).astype(F32)
    marks = jnp.concatenate([tokall[b0 + s, 192:193, :] for s in range(4)], axis=1)
    O4 = (r4 == marks).astype(F32)
    O4b = O4.astype(BF)
    th, tm, tl = split3(T)
    G4 = dotb(th, O4b, 1, 1) + dotb(tm, O4b, 1, 1) + dotb(tl, O4b, 1, 1)
    return G4, O4, Hs


def merge_kernel(hs_in, gt_in, idx_in, coef, basis, state, tok, tokall, M, Gown, ysrc, Y, A, S, X, Z, W0, W0S, UP0, SB0, HB0, UB0, U0,
                 UP, SB, HB, UB, U, VP, VB, V, KP, KB, K, CF, CSB, CHB, CB, SQ, SQB,
                 ag_s, ag_r, ag_l, ys, yr, bs, br, us, ur, us2, ur2, vs, vr, vs2, vr2, ks, kr, ks2, kr2, cs, cr, qs, qr, zs, zr):
    g = lax.axis_index("group"); d = lax.axis_index("dev")
    core = lax.rem(d, 2); p = d // 2
    sib = (g, 2 * p + 1 - core)
    sent = []
    def drain():
        @pl.when(g == 0)
        def _():
            for k in range(1, 8):
                rcopy(Z.at[ds8(0, 32)], Z.at[ds8(0, 32)], zs.at[k], zr.at[0], (g, d)).wait_send()
                rcopy(Z.at[ds8(0, 32)], Z.at[ds8(0, 32)], zs.at[16 + k], zr.at[0], (g, d)).wait_send()
        for c in sent:
            c.wait_send()
    AC = Axis(16, p, lambda i: (g, 2 * i + core), sent)
    AG = Axis(8, g, lambda i: (i, d), sent)
    b = pltpu.get_barrier_semaphore()
    AC.each(lambda k, q: pl.semaphore_signal(b, inc=1, device_id=AC.dev(q), device_id_type=MESH))
    AG.each(lambda k, q: pl.semaphore_signal(b, inc=1, device_id=AG.dev(q), device_id_type=MESH))
    pl.semaphore_signal(b, inc=1, device_id=sib, device_id_type=MESH)
    tok[0:128, :] = hs_in[...]
    tok[128:192, :] = gt_in[...]
    idx = idx_in[0:1, :]
    tok[192:200, :] = jnp.broadcast_to(idx + 32 * lax.rem(p, 4), (8, 128)).astype(F32)
    half = lambda c, n: pl.ds(pl.multiple_of(c * n, 8), n)
    hs_parts = split3(tok[0:128, :])
    h, m, l = split3(tok[128:192, :].T)
    gt_cat = jnp.concatenate([h, h, m, h, m, l], axis=1)
    drow = lax.broadcasted_iota(jnp.int32, (32, 128), 0)
    own = (jnp.broadcast_to(idx, (32, 128)) == drow).astype(BF)
    own3 = jnp.concatenate([own, own, own], axis=1)
    pl.semaphore_wait(b, 23)
    other_core = ag_tokens(g, d, tok, tokall, ag_s, ag_r, ag_l.at[3], sent)
    par = lax.rem(d, 4)
    gbase = pl.multiple_of((d // 4) * 8, 8)
    r8 = lax.broadcasted_iota(jnp.int32, (8, 128), 0)
    def four(q, c):
        G4, O4, Hs = token_blocks(hs_parts, gt_cat, own3, idx, tokall, 4 * q)
        Gown[q] = G4 * (1.0 / 8192)
        for s in range(4):
            g8 = tokall[4 * q + s, pl.ds(128 + gbase, 8), :]
            O1 = O4[32 * s:32 * s + 32, 128 * s:128 * s + 128]
            g0 = jnp.sum(jnp.where(r8 == 2 * par, g8, 0.0), axis=0, keepdims=True)
            g1 = jnp.sum(jnp.where(r8 == 2 * par + 1, g8, 0.0), axis=0, keepdims=True)
            wh, wm, wl = split3(jnp.concatenate([O1 * g0, O1 * g1], axis=0))
            h, m, l = Hs[s]
            mr = dotb(jnp.concatenate([wh, wh, wm, wh, wm, wl], axis=1), jnp.concatenate([h, m, h, l, m, h], axis=0)) * (1.0 / math.sqrt(8192))
            M[ds8(4 * q + s, 32), 0:128] = mr[0:32]
            M[ds8(4 * q + s, 32), 128:256] = mr[32:64]
        return c
    four(4 * core, 0)
    other_core()
    four(4 - 4 * core, 0)
    def later(i):
        def two(j, c):
            return four(4 * j + i + 1, c)
        lax.fori_loop(0, 2, two, 0)
    y0, y1 = Gown[0], Gown[4]
    ysrc[0] = jnp.concatenate([(y1 if s % 2 else y0)[:, 32 * (s // 2):32 * (s // 2) + 32] for s in range(8)], axis=1)
    for it in range(3):
        ag_block(g, d, ysrc.at[it], Y.at[it], ys.at[it], yr.at[it], ag_l.at[it], sent, later if it == 0 else lambda i: None)
        if it < 2:
            acc = jnp.zeros((32, 256), F32)
            for q in range(8):
                acc = acc + mm(Gown[q], Y[it, q // 4, q % 4].reshape(128, 256))
            ysrc[it + 1] = acc
    def zpart(q, acc):
        yb = Y[2, q // 2, pl.ds(2 * lax.rem(q, 2), 2)].reshape(256, 256)
        return acc + mm(yb, M[ds8(q, 256), :], 0, 0)
    def gram(q, acc):
        yb = Y[2, q // 2, pl.ds(2 * lax.rem(q, 2), 2)].reshape(256, 256)
        return acc + mm(yb, yb, 0, 0)
    zero = jnp.zeros((256, 256), F32)
    z1 = lax.fori_loop(0, 4, zpart, zero)
    Z[...] = z1
    @pl.when(g == 0)
    def _():
        for k in range(1, 8):
            rcopy(Z.at[ds8(k, 32)], X.at[ds8(k, 32)], zs.at[k], zr.at[0], (k, d)).start()
        X[0:32, :] = Z[0:32, :]
    A[...] = lax.fori_loop(0, 4, gram, zero)
    chol_inv_body(A, 0, 3)
    @pl.when(g > 0)
    def _():
        rcopy(X.at[ds8(g, 32)], X.at[ds8(g, 32)], zs.at[0], zr.at[0], (g, d)).wait_recv()
    AG.spread(X.at[ds8(g, 32)], X, 32, zs.at[pl.ds(8, 8)], zr.at[pl.ds(8, 8)])
    chol_inv_body(A, 3, 8)
    row = lax.broadcasted_iota(jnp.int32, (256, 256), 0); col = lax.broadcasted_iota(jnp.int32, (256, 256), 1)
    tri = col <= row
    diag = jnp.sum(jnp.where(col == row, A[...], 0.0), axis=0, keepdims=True)
    hi = jnp.max(diag, axis=1, keepdims=True); lo = jnp.min(diag, axis=1, keepdims=True)
    W = jnp.where(tri, A[...], 0.0) + jnp.where(hi < SPAN * lo, 0.0, jnp.nan)
    W0S[...] = W
    @pl.when(g == 0)
    def _():
        for k in range(1, 8):
            rcopy(W0S.at[ds8(k, 32)], W0.at[ds8(k, 32)], zs.at[16 + k], zr.at[16], (k, d)).start()
        W0[0:32, :] = W0S[0:32, :]
    S[...] = mm(W, z1)
    AG.collect(X, 32, zs.at[pl.ds(8, 8)], zr.at[pl.ds(8, 8)])
    xt = X[...].T
    def to_sibling(src, dst, i):
        c = rcopy(src, dst, bs.at[i], br.at[i], sib)
        c.start()
        sent.append(c)
        return c
    UP0[...] = mm(S[...], xt)
    first = to_sibling(UP0.at[half(1 - core, 128)], SB0, 0)
    @pl.when(g > 0)
    def _():
        rcopy(W0.at[ds8(g, 32)], W0.at[ds8(g, 32)], zs.at[0], zr.at[16], (g, d)).wait_recv()
    AG.spread(W0.at[ds8(g, 32)], W0, 32, zs.at[pl.ds(24, 8)], zr.at[pl.ds(24, 8)])
    first.wait_recv()
    HB0[...] = UP0[half(core, 128), :] + SB0[...]
    AC.scatter(HB0, UB0, us.at[4], ur.at[4])
    uh = U0.at[half(core, 128)]
    uh[ds8(p, 8), :] = AC.gather_sum(HB0, UB0, us.at[4], ur.at[4])
    AC.spread(uh.at[ds8(p, 8)], uh, 8, us2.at[4], ur2.at[4])
    AC.collect(uh, 8, us2.at[4], ur2.at[4])
    first = to_sibling(uh, uh, 1)
    AG.collect(W0, 32, zs.at[pl.ds(24, 8)], zr.at[pl.ds(24, 8)])
    first.wait_recv()
    u0 = mm(U0[...], W0[...], 1, 1)
    flying = {}
    def p1(it, h):
        j = 2 * it - 2 + h
        UP[j] = mm(S[...], V[2 * it - 2 + h])
        flying[j] = to_sibling(UP.at[j, half(1 - core, 128)], SB.at[j], 2 + 2 * j)
    def p2(it, h):
        j = 2 * it - 2 + h
        flying[j].wait_recv()
        HB[j] = UP[j, half(core, 128), :] + SB[j]
        AC.scatter(HB.at[j], UB.at[j], us.at[j], ur.at[j])
    def p3(it, h):
        j = 2 * it - 2 + h
        uh = U.at[j, half(core, 128)]
        uh[ds8(p, 8), :] = AC.gather_sum(HB.at[j], UB.at[j], us.at[j], ur.at[j])
        AC.spread(uh.at[ds8(p, 8)], uh, 8, us2.at[j], ur2.at[j])
    def p4(it, h):
        j = 2 * it - 2 + h
        uh = U.at[j, half(core, 128)]
        AC.collect(uh, 8, us2.at[j], ur2.at[j])
        flying[j] = to_sibling(uh, uh, 3 + 2 * j)
    def p5(it, h):
        v = 2 * it + h
        if it == 0:
            u = u0[:, 128 * h:128 * h + 128]
        else:
            if flying[v - 2] is not None:
                flying[v - 2].wait_recv()
            u = U[v - 2]
        VP[v] = mm(S[...], u, 0, 0)
        AG.scatter(VP.at[v], VB.at[v], vs.at[v], vr.at[v])
    def p6(it, h):
        v = 2 * it + h
        V[v, ds8(g, 32), :] = AG.gather_sum(VP.at[v], VB.at[v], vs.at[v], vr.at[v])
        AG.spread(V.at[v, ds8(g, 32)], V.at[v], 32, vs2.at[v], vr2.at[v])
    def p7(it, h):
        v = 2 * it + h
        AG.collect(V.at[v], 32, vs2.at[v], vr2.at[v])
    p5(0, 0); p5(0, 1); p6(0, 0); p6(0, 1); p7(0, 0)
    p1(1, 0); p2(1, 0); p3(1, 0); p4(1, 0); p7(0, 1)
    for n in range(3, 6):
        a, c = (n // 2, n % 2), ((n - 1) // 2, (n - 1) % 2)
        p1(*a); p5(*c); p2(*a); p3(*a); p6(*c); p4(*a)
        if n < 5:
            p7(*c)
    def coordinates(h):
        def cpart(q, c):
            CF[h, ds8(q, 256), :] = mm(M[ds8(q, 256), :], V[4 + h])
            return c
        lax.fori_loop(0, 4, cpart, 0)
        return to_sibling(CF.at[h, half(1 - core, 512)], CSB.at[h], 11 + h)
    def coordinates_out(h, c):
        c.wait_recv()
        CHB[h] = CF[h, half(core, 512), :] + CSB[h]
        AC.scatter(CHB.at[h], CB.at[h], cs.at[h], cr.at[h])
    mine = core * 16 + p
    flying[3].wait_recv()
    flying[3] = None
    u = jnp.concatenate([U[2], U[3]], axis=1)
    KP[...] = mm(u, u, 0, 0)
    KB[ds8(g, 8), :] = KP[ds8(mine, 8), :]
    AG.spread(KP.at[ds8(mine, 8)], KB, 8, ks, kr)
    p5(2, 1)
    AG.collect(KB, 8, ks, kr)
    acc = KB[0:8, :]
    for q in range(1, 8):
        acc = acc + KB[8 * q:8 * q + 8, :]
    kh = K.at[half(core, 128)]
    kh[ds8(p, 8), :] = acc
    AC.spread(kh.at[ds8(p, 8)], kh, 8, ks2, kr2)
    p7(2, 0)
    c0 = coordinates(0)
    p6(2, 1)
    AC.collect(kh, 8, ks2, kr2)
    swap_k = to_sibling(kh, kh, 10)
    coordinates_out(0, c0)
    swap_k.wait_recv()
    A[...] = K[...]
    chol_inv_body(A, 0, 3)
    p7(2, 1)
    c1 = coordinates(1)
    chol_inv_body(A, 3, 5)
    coordinates_out(1, c1)
    chol_inv_body(A, 5, 8)
    diag = jnp.sum(jnp.where(col == row, A[...], 0.0), axis=0, keepdims=True)
    hi = jnp.max(diag, axis=1, keepdims=True); lo = jnp.min(diag, axis=1, keepdims=True)
    state[0, 0] = jnp.max(jnp.where(hi < SPAN * lo, 1.0, 0.0))
    W = jnp.where(tri, A[...], 0.0)
    mt = mm(jnp.concatenate([V[4], V[5]], axis=1), W, 1, 1)
    SQ[0] = jnp.broadcast_to(jnp.sum(mt * mt, axis=0, keepdims=True), (8, 256))
    qsib = rcopy(SQ.at[0], SQ.at[1], qs.at[0], qr.at[0], sib)
    qsib.start()
    sent.append(qsib)
    qsib.wait_recv()
    SQB[ds8(p, 8), :] = SQ[0] + SQ[1]
    AC.spread(SQB.at[ds8(p, 8)], SQB, 8, qs, qr)
    cfs = mm(jnp.concatenate([AC.gather_sum(CHB.at[h], CB.at[h], cs.at[h], cr.at[h]) for h in range(2)], axis=1), W, 1, 1)
    AC.collect(SQB, 8, qs, qr)
    sq = SQB[0:8, :]
    for q in range(1, 16):
        sq = sq + SQB[8 * q:8 * q + 8, :]
    f = 1.0 / jnp.sqrt(sq[0:1, :] / 8192.0 + 1e-06)
    coef[...] = cfs * (f * (1.0 / math.sqrt(8192)))
    basis[...] = (mt * f).T
    drain()


def merge_all(hs, gt, idx):
    D = pltpu.SemaphoreType.DMA
    V = lambda *s: pltpu.VMEM(s, F32)
    return pl.pallas_call(
        merge_kernel,
        out_shape=[jax.ShapeDtypeStruct((32, 256), F32), jax.ShapeDtypeStruct((256, 256), F32), jax.ShapeDtypeStruct((1, 1), F32)],
        in_specs=[VM, VM, VM], out_specs=[VM, VM, pl.BlockSpec(memory_space=pltpu.SMEM)],
        scratch_shapes=[
            V(200, 128), V(32, 200, 128), V(1024, 256), V(8, 32, 128), V(3, 32, 256), V(3, 2, 4, 4, 32, 256),
            V(256, 256), V(256, 256), V(256, 256), V(256, 256), V(256, 256), V(256, 256),
            V(256, 256), V(128, 256), V(128, 256), V(16, 8, 256), V(256, 256),
            V(4, 256, 128), V(4, 128, 128), V(4, 128, 128), V(4, 16, 8, 128), V(4, 256, 128),
            V(6, 256, 128), V(6, 8, 32, 128), V(6, 256, 128),
            V(256, 256), V(64, 256), V(256, 256),
            V(2, 1024, 128), V(2, 512, 128), V(2, 512, 128), V(2, 16, 32, 128), V(2, 8, 256), V(128, 256),
            D((80,)), D((32, 2)), D((4,)), D((3, 16)), D((3, 16)), D((16,)), D((16,)),
            D((5, 16)), D((5, 16)), D((5, 16)), D((5, 16)), D((6, 8)), D((6, 8)), D((6, 8)), D((6, 8)),
            D((8,)), D((8,)), D((16,)), D((16,)), D((2, 16)), D((2, 16)), D((16,)), D((16,)), D((32,)), D((32,)),
        ],
        compiler_params=pltpu.CompilerParams(collective_id=1, has_side_effects=True, vmem_limit_bytes=56 << 20),
    )(hs, gt, idx)


def merge_slow(hs, gt, doc_index):
    def orth(Y):
        return mm(Y, chol_inv(mm(Y, Y, 0, 0)), 1, 1)
    def sum_parts(x, axis, n):
        r = x.shape[0] // n
        return lax.all_to_all(x, axis, split_axis=0, concat_axis=0, tiled=True).reshape(n, r, x.shape[1]).sum(axis=0)
    def gather(x, axis, n):
        return lax.all_to_all(jnp.tile(x, (n, 1)), axis, split_axis=0, concat_axis=0, tiled=True)
    def total(x):
        return gather(sum_parts(x, "dev", 32), "dev", 32)
    own = (doc_index == jnp.arange(DOC_DEV, dtype=jnp.int32)[:, None]).astype(F32)
    weighted = own[:, None, :] * gt[None, :, :]
    rows = mm(weighted.reshape(-1, 128), hs).reshape(DOC_DEV, 8192) * (1.0 / math.sqrt(8192))
    block = lax.all_to_all(rows, "dev", split_axis=1, concat_axis=0, tiled=True)
    G = total(mm(block, block, 1, 1))
    Q = lax.fori_loop(0, ITERS + 1, lambda _, Q: orth(mm(G, Q)), jnp.eye(1024, RANK, dtype=F32))
    stacked = gather(mm(Q, block, 0, 0), "group", 8)
    Q = lax.fori_loop(0, ITERS + 1, lambda _, Q: orth(total(mm(stacked, mm(stacked, Q, 0, 0)))), jnp.eye(2048, RANK, dtype=F32))
    merged = mm(Q, stacked, 0, 0)
    squares = total(jnp.broadcast_to(jnp.sum(merged * merged, axis=1)[None, :], (32, RANK)))[0]
    basis = merged * (1.0 / jnp.sqrt(squares / 8192.0 + 1e-06))[:, None]
    summed = sum_parts(mm(block, basis, 1, 1), "dev", 32)
    return summed / math.sqrt(8192), basis


def on_device(hidden_acts, out_grads, doc_index, proj_hidden, proj_grad):
    hs = lax.dot_general(hidden_acts, proj_hidden, (((1,), (1,)), ((), ())), preferred_element_type=F32)
    gt = lax.dot_general(proj_grad, out_grads, (((1,), (1,)), ((), ())), preferred_element_type=F32)
    coef, basis, state = merge_all(hs, gt, doc_index)
    return lax.cond(state[0, 0] > 0.5, lambda: (coef, basis), lambda: merge_slow(hs, gt, doc_index))


def solution(mesh):
    return jax.shard_map(
        on_device,
        mesh=mesh,
        in_specs=(
            P(("group", "dev"), None),
            P(("group", "dev"), None),
            P(("group", "dev"), None),
            P(),
            P(),
        ),
        out_specs=(P(("group", "dev"), None), P(None, "dev")),
        check_vma=False,
    )
```
